32 devices in a mesh: row: 8 (over y, x, core), col: 4 (over z).
Axes of the slice: x: 2, y: 2, z: 4, core: 2. Of those that a mesh axis runs over, the one named last changes fastest.
Arguments:
- left_blocks: bfloat16 [8, 4, 64, 529], P('row', 'col'), may hold values from -1.1953125 to 1.1953125
- left_rows: int32 [8, 4, 64], P('row'), may hold values from 0 to 15
- left_cols: int32 [8, 4, 64], P('row'), may hold values from 0 to 15
- left_counts: int32 [8, 4], P('row'), may hold values from 32 to 64, as said below
- right_blocks: bfloat16 [8, 4, 128, 529], P('row', 'col'), may hold values from -6 to 6
- right_cols: int32 [8, 4, 16, 8], P(None, 'col'), may hold values from 0 to 31, as said below
Outputs:
- product: float32 [8, 4, 512, 529], P('row', 'col')
The draws below stay inside these ranges and needn't reach their ends.
Inputs may be any that keep to these rules, and one draw needn't show every extreme that they name: `left_counts`: every count lies between 32 and 64, and some left panel is full in every draw. `right_cols`: the 8 block columns of one inner block row of one right panel are distinct.
All inputs are finite; a program needn't handle non-finite values.
Results may differ from the reference program's by a relative error of at most 0.0003.
Values may be sent and summed in bfloat16 or wider, within the bound.
No kernel may reach another device: no remote copies, remote signals or barrier semaphores. Data moves between devices by JAX's collectives and lax.ppermute only.
A program may use at most 64 MiB of HBM per device.

```python
import jax
import jax.numpy as jnp
from jax import lax

BS = 23
RB = 16
CB = 32
KB = 16
SA = 64
BPK = 8
N_ROW = 8
N_COL = 4


def draw_left_counts(key, part):
    key = jax.random.fold_in(key, 11)
    counts = jax.random.randint(key, (N_ROW * N_COL,), SA // 2, SA + 1)
    chosen = jax.random.randint(jax.random.fold_in(key, 1), (), 0, N_ROW * N_COL)
    counts = jnp.where(jnp.arange(N_ROW * N_COL) == chosen, SA, counts)
    return counts.reshape(N_ROW, N_COL).astype(jnp.int32)


def draw_right_cols(key, part):
    key = jax.random.fold_in(key, 12)
    scores = jax.random.randint(key, (N_ROW, N_COL, KB, CB), 0, 1 << 20) * CB + jnp.arange(CB)
    order = jnp.argsort(scores, axis=-1, stable=True)[..., :BPK]
    return order.astype(jnp.int32)


def with_ends(drawn, rng, smallest, largest):
    index_at = [jax.random.randint(jax.random.fold_in(rng, axis), (), 0, length) for axis, length in enumerate(drawn.shape)]
    widest = drawn.shape.index(max(drawn.shape))
    beside = index_at[:widest] + [(index_at[widest] + 1) % drawn.shape[widest]] + index_at[widest + 1:]
    return drawn.at[tuple(index_at)].set(smallest).at[tuple(beside)].set(largest)


def block_scale(rng, extent, cuts, low, top_value):
    gain = 1.0
    for position, blocks in cuts:
        draws = jax.random.uniform(jax.random.fold_in(jax.random.fold_in(rng, 6), position), (blocks,), jnp.float32, low / len(cuts), top_value / len(cuts))
        gain = gain * jnp.repeat(jnp.exp(draws), extent[position] // blocks).reshape((-1,) + (1,) * (len(extent) - 1 - position))
    return gain


def normal_values(rng, extent, width, bound, pieces=(), kind=jnp.bfloat16):
    level = block_scale(rng, extent, pieces, -0.22, 0.18) if pieces else 1.0
    drawn = jax.random.normal(rng, extent, jnp.float32) * width * level
    return jnp.minimum(jnp.maximum(drawn, -bound), bound).astype(kind)


def setup_inputs(seed: int = 0) -> dict:
    arg_keys = jax.random.split(jax.random.key(seed), 7)
    left_blocks = normal_values(arg_keys[0], (N_ROW, N_COL, SA, BS * BS), 0.2, 1.1953125, ((0, 8), (1, 4)))
    left_rows = with_ends(jax.random.randint(arg_keys[1], (N_ROW, N_COL, SA), 0, RB), jax.random.fold_in(arg_keys[1], 1), 0, RB - 1).astype(jnp.int32)
    left_cols = with_ends(jax.random.randint(arg_keys[2], (N_ROW, N_COL, SA), 0, KB), jax.random.fold_in(arg_keys[2], 1), 0, KB - 1).astype(jnp.int32)
    left_counts = draw_left_counts(jax.random.fold_in(arg_keys[6], 71), 0)
    right_blocks = normal_values(arg_keys[4], (N_ROW, N_COL, KB * BPK, BS * BS), 1.0, 6.0, ((0, 8), (1, 4)))
    right_cols = draw_right_cols(jax.random.fold_in(arg_keys[6], 71), 0)
    return dict(left_blocks=left_blocks, left_rows=left_rows, left_cols=left_cols, left_counts=left_counts, right_blocks=right_blocks, right_cols=right_cols)


def panel_term(blocks, rows, cols, count, kblocks, kcols):
    slots = blocks.shape[0]
    left_mats = blocks.reshape(slots, BS, BS).astype(jnp.float32)
    right_mats = kblocks.reshape(KB, BPK, BS, BS)[cols].astype(jnp.float32)
    products = jnp.einsum("sij,srjk->srik", left_mats, right_mats)
    keep = (jnp.arange(slots) < count).astype(jnp.float32)
    products = products * keep[:, None, None, None]
    target = (rows[:, None] * CB + kcols[cols]).astype(jnp.int32)
    return jax.ops.segment_sum(products.reshape(slots * BPK, BS * BS), target.reshape(-1), num_segments=RB * CB)


def reference(left_blocks, left_rows, left_cols, left_counts, right_blocks, right_cols):
    total = jnp.zeros((N_ROW, N_COL, RB * CB, BS * BS), jnp.float32)
    for offset in range(3):
        moved = (
            jnp.roll(left_blocks, -offset, axis=1),
            jnp.roll(left_rows, -offset, axis=1),
            jnp.roll(left_cols, -offset, axis=1),
            jnp.roll(left_counts, -offset, axis=1),
            jnp.roll(right_blocks, -offset, axis=0),
            jnp.roll(right_cols, -offset, axis=0),
        )

        def one_row(items):
            return jax.vmap(panel_term)(*items)

        total = total + lax.map(one_row, moved)
    return total
```

```python
import functools
import jax
import jax.numpy as jnp
from jax import lax
from jax.experimental import pallas as pl
from jax.experimental.pallas import tpu as pltpu
from jax.sharding import PartitionSpec as P

BS = 23
RB = 16
CB = 32
KB = 16
BPK = 8
SA = 64
JP = 32
QUADS = 6
NB = BS * BS
F32 = jnp.float32
BF16 = jnp.bfloat16


def from_behind(value, axis, by):
    devices = lax.axis_size(axis)
    return lax.ppermute(value, axis, [(i, (i + by) % devices) for i in range(devices)])


def swap_quads(v):
    lane = lax.broadcasted_iota(jnp.int32, v[0].shape, 1)
    half = lane < 64
    even = (lane & 32) == 0
    w = [None] * 4
    for a in (0, 1):
        w[a] = jnp.where(half, v[a], pltpu.roll(v[a + 2], 64, 1))
        w[a + 2] = jnp.where(half, pltpu.roll(v[a], 64, 1), v[a + 2])
    z = [None] * 4
    for a in (0, 2):
        z[a] = jnp.where(even, w[a], pltpu.roll(w[a + 1], 32, 1))
        z[a + 1] = jnp.where(even, pltpu.roll(w[a], 96, 1), w[a + 1])
    return z


def spread_matrix(t_ref):
    lane = lax.broadcasted_iota(jnp.int32, (1, QUADS * 128), 1)
    i, j = lane >> 5, lane & 31
    source = jnp.where((j < BS) & (i < BS), i * BS + j, -1)
    entry = lax.broadcasted_iota(jnp.int32, (NB, QUADS * 128), 0)
    t_ref[...] = jnp.where(entry == source, 1.0, 0.0).astype(BF16)


def left_panel(blocks, rows, cols, count, t_ref, a_ref, base):
    wide = jnp.dot(blocks, t_ref[...], preferred_element_type=F32).astype(BF16)
    slot = lax.broadcasted_iota(jnp.int32, (1, SA), 1)
    code = jnp.where(slot < count, cols * RB + rows, -1)
    place = lax.broadcasted_iota(jnp.int32, (KB * RB, SA), 0)
    pick = jnp.where(place == code, 1.0, 0.0).astype(BF16)
    for q in range(QUADS):
        sums = jnp.dot(pick, wide[:, q * 128 : (q + 1) * 128], preferred_element_type=F32)
        for g in range(KB // 4):
            v = [sums[(4 * g + a) * RB : (4 * g + a + 1) * RB] for a in range(4)]
            for a, z in enumerate(swap_quads(v)):
                i = 4 * q + a
                if i < BS:
                    hi = z.astype(BF16)
                    lo = (z - hi.astype(F32)).astype(BF16)
                    at = base + g * 128
                    a_ref[i * RB : (i + 1) * RB, at : at + 128] = hi
                    a_ref[(BS + i) * RB : (BS + i + 1) * RB, at : at + 128] = lo


def right_panel(blocks, cols, w_ref, b_ref, base):
    w_ref[528:552, :] = jnp.zeros((24, 128), F32)
    w_ref[0:NB, :] = blocks.astype(F32)
    lane = lax.broadcasted_iota(jnp.int32, (BPK, 128), 1)
    none = jnp.zeros((BPK, 128), F32)
    spread = []
    for kap in range(KB):
        one = jnp.where(lane - 32 * (kap % 4) == cols[:, kap : kap + 1], 1.0, 0.0)
        spread.append(jnp.concatenate([one if g == kap // 4 else none for g in range(4)], axis=1))
    spread = jnp.concatenate(spread, axis=0).astype(BF16)
    pad = jnp.zeros((8, 128), F32)
    for q in range(QUADS):
        entries = []
        for a in range(4):
            k = 4 * q + a
            if k < BS:
                entries += [w_ref[pl.ds(k, 24, stride=BS), :], pad]
            else:
                entries += [pad] * 4
        entries = jnp.concatenate(entries, axis=0).astype(BF16)
        full = jnp.dot(entries, spread, preferred_element_type=F32)
        for g in range(4):
            v = [full[a * JP : (a + 1) * JP, g * 128 : (g + 1) * 128] for a in range(4)]
            for a, z in enumerate(swap_quads(v)):
                at = base + (4 * g + a) * JP
                b_ref[at : at + JP, q * 128 : (q + 1) * 128] = z.astype(BF16)


def kernel(counts_ref, l0, l1, l2, rows_ref, cols_ref, r0, r1, r2, kcols_ref, out_ref,
           t_ref, a_ref, w_ref, b_ref, p_ref):
    ncol, nrow = rows_ref.shape[1], kcols_ref.shape[0]
    spread_matrix(t_ref)
    for s, (l, r) in enumerate(((l0, r0), (l1, r1), (l2, r2))):
        panel = lax.rem(lax.axis_index("col") + s, ncol)
        source = lax.rem(lax.axis_index("row") + s, nrow)
        rows = rows_ref[0, pl.ds(panel, 1), :]
        cols = cols_ref[0, pl.ds(panel, 1), :]
        left_panel(l[...], rows, cols, counts_ref[0, panel], t_ref, a_ref, s * 512)
        right_panel(r[...], kcols_ref[source], w_ref, b_ref, s * 512)
    for q in range(QUADS):
        lanes = slice(q * 128, (q + 1) * 128)
        both = jnp.dot(a_ref[...], b_ref[:, lanes], preferred_element_type=F32)
        for i in range(BS):
            total = both[i * RB : (i + 1) * RB] + both[(BS + i) * RB : (BS + i + 1) * RB]
            p_ref[q, pl.ds(i, RB, stride=24), :] = total
    for rq in range(RB // 4):
        for ib in range(3):
            for q in range(QUADS):
                v = [p_ref[q, (4 * rq + a) * 24 + ib * 8 : (4 * rq + a) * 24 + ib * 8 + 8, :] for a in range(4)]
                for a, z in enumerate(swap_quads(v)):
                    k = 4 * q + a
                    n = 8 if ib < 2 else 7
                    if k < BS:
                        out_ref[pl.ds((ib * 8 * BS + k) * 4 + rq, n, stride=4 * BS), :] = z[:n]


def body(left_blocks, left_rows, left_cols, left_counts, right_blocks, right_cols):
    left = left_blocks[0, 0]
    right = jnp.swapaxes(right_blocks[0, 0], 0, 1)
    kcols = jnp.swapaxes(right_cols[:, 0], 1, 2)
    l1, l2 = from_behind(left, "col", -1), from_behind(left, "col", -2)
    r1, r2 = from_behind(right, "row", -1), from_behind(right, "row", -2)
    vmem = pl.BlockSpec(memory_space=pltpu.VMEM)
    out = pl.pallas_call(
        kernel,
        out_shape=jax.ShapeDtypeStruct((NB * 4, 128), F32),
        in_specs=[pl.BlockSpec(memory_space=pltpu.SMEM)] + [vmem] * 9,
        out_specs=vmem,
        scratch_shapes=[
            pltpu.VMEM((NB, QUADS * 128), BF16),
            pltpu.VMEM((2 * BS * RB, 3 * 512), BF16),
            pltpu.VMEM((552, 128), F32),
            pltpu.VMEM((3 * 512, QUADS * 128), BF16),
            pltpu.VMEM((QUADS, RB * 24, 128), F32),
        ],
        compiler_params=pltpu.CompilerParams(vmem_limit_bytes=32 * 1024 * 1024),
    )(left_counts, left, l1, l2, left_rows, left_cols, right, r1, r2, kcols)
    return jnp.swapaxes(out.reshape(NB, RB * CB), 0, 1)[None, None]


def solution(mesh):
    in_specs = (
        P("row", "col", None, None),
        P("row", None, None),
        P("row", None, None),
        P("row", None),
        P("row", "col", None, None),
        P(None, "col", None, None),
    )
    out_specs = P("row", "col", None, None)
    return jax.shard_map(body, mesh=mesh, in_specs=in_specs, out_specs=out_specs, check_vma=False)
```

```python
import functools
import jax
import jax.numpy as jnp
from jax import lax
from jax.experimental import pallas as pl
from jax.experimental.pallas import tpu as pltpu
from jax.sharding import PartitionSpec as P

BS = 23
RB = 16
CB = 32
KB = 16
BPK = 8
SA = 64
JP = 32
QUADS = 6
NB = BS * BS
WIDE = QUADS * 128
DEPTH = KB * JP
F32 = jnp.float32
BF16 = jnp.bfloat16


def from_behind(value, axis, by):
    devices = lax.axis_size(axis)
    return lax.ppermute(value, axis, [(i, (i + by) % devices) for i in range(devices)])


def swap_quads(v):
    lane = lax.broadcasted_iota(jnp.int32, v[0].shape, 1)
    half = lane < 64
    even = (lane & 32) == 0
    w = [None] * 4
    for a in (0, 1):
        w[a] = jnp.where(half, v[a], pltpu.roll(v[a + 2], 64, 1))
        w[a + 2] = jnp.where(half, pltpu.roll(v[a], 64, 1), v[a + 2])
    z = [None] * 4
    for a in (0, 2):
        z[a] = jnp.where(even, w[a], pltpu.roll(w[a + 1], 32, 1))
        z[a + 1] = jnp.where(even, pltpu.roll(w[a], 96, 1), w[a + 1])
    return z


def spread_matrix(t_ref):
    lane = lax.broadcasted_iota(jnp.int32, (1, WIDE), 1)
    i, j = lane >> 5, lane & 31
    source = jnp.where((j < BS) & (i < BS), i * BS + j, -1)
    entry = lax.broadcasted_iota(jnp.int32, (NB, WIDE), 0)
    t_ref[...] = jnp.where(entry == source, 1.0, 0.0).astype(BF16)


def slot_pick(rows, cols, count):
    slot = lax.broadcasted_iota(jnp.int32, (1, SA), 1)
    code = jnp.where(slot < count, cols * RB + rows, -1)
    place = lax.broadcasted_iota(jnp.int32, (KB * RB, SA), 0)
    return jnp.where(place == code, 1.0, 0.0).astype(BF16)


def column_spread(cols):
    lane = lax.broadcasted_iota(jnp.int32, (BPK, 128), 1)
    none = jnp.zeros((BPK, 128), F32)
    spread = []
    for kap in range(KB):
        one = jnp.where(lane - 32 * (kap % 4) == cols[:, kap : kap + 1], 1.0, 0.0)
        spread.append(jnp.concatenate([one if g == kap // 4 else none for g in range(4)], axis=1))
    return jnp.concatenate(spread, axis=0).astype(BF16)


def left_panel(blocks, pick, t_ref, a_ref, base):
    wide = jnp.dot(blocks, t_ref[...], preferred_element_type=F32).astype(BF16)
    for q in range(QUADS):
        sums = jnp.dot(pick, wide[:, q * 128 : (q + 1) * 128], preferred_element_type=F32)
        for g in range(KB // 4):
            v = [sums[(4 * g + a) * RB : (4 * g + a + 1) * RB] for a in range(4)]
            for a, z in enumerate(swap_quads(v)):
                i = 4 * q + a
                if i < BS:
                    hi = z.astype(BF16)
                    lo = (z - hi.astype(F32)).astype(BF16)
                    at = base + g * 128
                    a_ref[i * RB : (i + 1) * RB, at : at + 128] = hi
                    a_ref[(BS + i) * RB : (BS + i + 1) * RB, at : at + 128] = lo


def right_panel(blocks, spread, w_ref, b_ref, base):
    w_ref[528:552, :] = jnp.zeros((24, 128), F32)
    w_ref[0:NB, :] = blocks.astype(F32)
    pad = jnp.zeros((8, 128), F32)
    for q in range(QUADS):
        entries = []
        for a in range(4):
            k = 4 * q + a
            if k < BS:
                entries += [w_ref[pl.ds(k, 24, stride=BS), :], pad]
            else:
                entries += [pad] * 4
        entries = jnp.concatenate(entries, axis=0).astype(BF16)
        full = jnp.dot(entries, spread, preferred_element_type=F32)
        for g in range(4):
            v = [full[a * JP : (a + 1) * JP, g * 128 : (g + 1) * 128] for a in range(4)]
            for a, z in enumerate(swap_quads(v)):
                at = base + (4 * g + a) * JP
                b_ref[at : at + JP, q * 128 : (q + 1) * 128] = z.astype(BF16)


def multiply(a_ref, b_ref, p_ref):
    for q in range(QUADS):
        both = jnp.dot(a_ref[...], b_ref[:, q * 128 : (q + 1) * 128], preferred_element_type=F32)
        for i in range(BS):
            total = both[i * RB : (i + 1) * RB] + both[(BS + i) * RB : (BS + i + 1) * RB]
            p_ref[q, pl.ds(i, RB, stride=24), :] = total


def first_kernel(counts_hbm, rows_hbm, cols_hbm, kcols_hbm, l_hbm, r_hbm,
                 p_ref, t_ref, pick_ref, spread_ref,
                 counts, rows, cols, kcols, l_ref, r_ref, a_ref, w_ref, b_ref, sems):
    moves = [
        pltpu.make_async_copy(s, d, sems.at[n])
        for n, (s, d) in enumerate((
            (counts_hbm, counts), (rows_hbm, rows), (cols_hbm, cols), (kcols_hbm, kcols),
            (l_hbm, l_ref), (r_hbm, r_ref),
        ))
    ]
    for move in moves:
        move.start()
    spread_matrix(t_ref)
    for move in moves:
        move.wait()
    ncol, nrow = rows.shape[1], kcols.shape[0]
    for s in range(3):
        panel = lax.rem(lax.axis_index("col") + s, ncol)
        source = lax.rem(lax.axis_index("row") + s, nrow)
        pick_ref[s] = slot_pick(rows[0, pl.ds(panel, 1), :], cols[0, pl.ds(panel, 1), :], counts[0, panel])
        spread_ref[s] = column_spread(kcols[source])
    left_panel(l_ref[...], pick_ref[0], t_ref, a_ref, 0)
    right_panel(r_ref[...], spread_ref[0], w_ref, b_ref, 0)
    multiply(a_ref, b_ref, p_ref)


def left_kernel(l1, l2, t_ref, pick_ref, a_ref):
    left_panel(l1[...], pick_ref[1], t_ref, a_ref, 0)
    left_panel(l2[...], pick_ref[2], t_ref, a_ref, DEPTH)


def last_kernel(a_ref, r1, r2, spread_ref, first_ref, out_hbm, w_ref, b_ref, p_ref, o_ref, sems):
    right_panel(r1[...], spread_ref[1], w_ref, b_ref, 0)
    right_panel(r2[...], spread_ref[2], w_ref, b_ref, DEPTH)
    multiply(a_ref, b_ref, p_ref)
    out = out_hbm.reshape(NB * 4, 128)
    moves = []
    for ib in range(3):
        n = 8 if ib < 2 else 7
        for rq in range(RB // 4):
            for q in range(QUADS):
                at = [(4 * rq + a) * 24 + ib * 8 for a in range(4)]
                v = [p_ref[q, t : t + 8, :] + first_ref[q, t : t + 8, :] for t in at]
                for a, z in enumerate(swap_quads(v)):
                    k = 4 * q + a
                    if k < BS:
                        o_ref[pl.ds((ib * 8 * BS + k) * 4 + rq, n, stride=4 * BS), :] = z[:n]
        part = pl.ds(ib * 8 * BS * 4, n * BS * 4)
        moves.append(pltpu.make_async_copy(o_ref.at[part], out.at[part], sems.at[ib]))
        moves[-1].start()
    for move in moves:
        move.wait()


VMEM = pl.BlockSpec(memory_space=pltpu.VMEM)
ANY = pl.BlockSpec(memory_space=pl.ANY)
LIMIT = pltpu.CompilerParams(vmem_limit_bytes=24 * 1024 * 1024)


def shape(*dims, dtype=F32):
    return jax.ShapeDtypeStruct(dims, dtype)


def body(left_blocks, left_rows, left_cols, left_counts, right_blocks, right_cols):
    left = left_blocks[0, 0]
    right = jnp.swapaxes(right_blocks[0, 0], 0, 1)
    kcols = jnp.swapaxes(right_cols[:, 0], 1, 2)
    l2, l1 = from_behind(left, "col", -2), from_behind(left, "col", -1)
    r2, r1 = from_behind(right, "row", -2), from_behind(right, "row", -1)
    first, spread_t, pick, spread = pl.pallas_call(
        first_kernel,
        out_shape=(shape(QUADS, RB * 24, 128), shape(NB, WIDE, dtype=BF16),
                   shape(3, KB * RB, SA, dtype=BF16), shape(3, KB * BPK, KB * CB, dtype=BF16)),
        in_specs=[ANY] * 6,
        out_specs=(VMEM,) * 4,
        scratch_shapes=[
            pltpu.SMEM(left_counts.shape, jnp.int32),
            pltpu.VMEM(left_rows.shape, jnp.int32),
            pltpu.VMEM(left_cols.shape, jnp.int32),
            pltpu.VMEM(kcols.shape, jnp.int32),
            pltpu.VMEM((SA, NB), BF16),
            pltpu.VMEM((NB, 128), BF16),
            pltpu.VMEM((2 * BS * RB, DEPTH), BF16),
            pltpu.VMEM((552, 128), F32),
            pltpu.VMEM((DEPTH, WIDE), BF16),
            pltpu.SemaphoreType.DMA((6,)),
        ],
        compiler_params=LIMIT,
        cost_estimate=pl.CostEstimate(flops=1, bytes_accessed=1, transcendentals=0),
    )(*(pltpu.with_memory_space_constraint(x, pltpu.HBM) for x in (left_counts, left_rows, left_cols, kcols, left, right)))
    dense = pl.pallas_call(
        left_kernel,
        out_shape=shape(2 * BS * RB, 2 * DEPTH, dtype=BF16),
        in_specs=[VMEM] * 4,
        out_specs=VMEM,
        compiler_params=LIMIT,
        cost_estimate=pl.CostEstimate(flops=10**10, bytes_accessed=4 * 10**6, transcendentals=0),
    )(l1, l2, spread_t, pick)
    out = pl.pallas_call(
        last_kernel,
        out_shape=shape(NB, 1, RB * CB),
        in_specs=[VMEM] * 5,
        out_specs=ANY,
        scratch_shapes=[
            pltpu.VMEM((552, 128), F32),
            pltpu.VMEM((2 * DEPTH, WIDE), BF16),
            pltpu.VMEM((QUADS, RB * 24, 128), F32),
            pltpu.VMEM((2120, 128), F32),
            pltpu.SemaphoreType.DMA((3,)),
        ],
        compiler_params=LIMIT,
        cost_estimate=pl.CostEstimate(flops=10**9, bytes_accessed=8 * 10**6, transcendentals=0),
    )(dense, r1, r2, spread, first)
    return jnp.transpose(out[None], (0, 2, 3, 1))


def solution(mesh):
    in_specs = (
        P("row", "col", None, None),
        P("row", None, None),
        P("row", None, None),
        P("row", None),
        P("row", "col", None, None),
        P(None, "col", None, None),
    )
    out_specs = P("row", "col", None, None)
    return jax.shard_map(body, mesh=mesh, in_specs=in_specs, out_specs=out_specs, check_vma=False)
```

```python
import jax
import jax.numpy as jnp
from jax import lax
from jax.experimental import pallas as pl
from jax.experimental.pallas import tpu as pltpu
from jax.sharding import PartitionSpec as P

BS = 23
RB = 16
CB = 32
KB = 16
BPK = 8
SA = 64
JP = 32
QUADS = 6
NB = BS * BS
ROWS = BS * RB
WIDE = QUADS * 128
DEPTH = KB * JP
BANDS = ((0, 256), (128, 384), (256, NB))
F32 = jnp.float32
BF16 = jnp.bfloat16


def from_behind(value, axis, by):
    devices = lax.axis_size(axis)
    return lax.ppermute(value, axis, [(i, (i + by) % devices) for i in range(devices)])


def lanes_like(v):
    return lax.broadcasted_iota(jnp.int32, v.shape, 1)


def unrotate(v, shift):
    chunk = lanes_like(v[0]) >> 5
    z = v[(3 - shift) % 4]
    for p in range(3):
        z = jnp.where(chunk == p, v[(p - shift) % 4], z)
    return pltpu.roll(z, 128 - 32 * shift, 1) if shift else z


def spread_matrix(t_ref):
    for u, (start, stop) in enumerate(BANDS):
        lane = lax.broadcasted_iota(jnp.int32, (1, 256), 1) + 256 * u
        i, j = lane >> 5, lane & 31
        source = jnp.where((j < BS) & (i < BS), i * BS + j, -1)
        entry = lax.broadcasted_iota(jnp.int32, (stop - start, 256), 0) + start
        t_ref[start:stop, 256 * u : 256 * (u + 1)] = jnp.where(entry == source, 1.0, 0.0).astype(BF16)


def slot_pick(rows, cols, count):
    slot = lax.broadcasted_iota(jnp.int32, (1, SA), 1)
    code = (cols & 3) * 64 + (cols >> 2) * RB + rows
    code = jnp.where(slot < count, code, -1)
    place = lax.broadcasted_iota(jnp.int32, (KB * RB, SA), 0)
    return jnp.where(place == code, 1.0, 0.0).astype(BF16)


def column_spread(cols, turn):
    lane = lax.broadcasted_iota(jnp.int32, (BPK, 128), 1)
    none = jnp.zeros((BPK, 128), F32)
    spread = []
    for kap in range(KB):
        one = jnp.where(lane - 32 * ((kap + turn) % 4) == cols[:, kap : kap + 1], 1.0, 0.0)
        spread.append(jnp.concatenate([one if g == kap // 4 else none for g in range(4)], axis=1))
    return jnp.concatenate(spread, axis=0).astype(BF16)


def left_panel(l_ref, pick, t_ref, a_ref):
    for u, (start, stop) in enumerate(BANDS):
        wide = jnp.dot(l_ref[:, start:stop], t_ref[start:stop, 256 * u : 256 * (u + 1)], preferred_element_type=F32)
        sums = []
        for a in range(4):
            turned = wide
            if a:
                turned = jnp.concatenate([pltpu.roll(wide[:, h : h + 128], 32 * a, 1) for h in (0, 128)], axis=1)
            sums.append(jnp.dot(pick[64 * a : 64 * (a + 1)], turned.astype(BF16), preferred_element_type=F32))
        for h in range(2):
            for g in range(KB // 4):
                v = [s[g * RB : (g + 1) * RB, h * 128 : (h + 1) * 128] for s in sums]
                for a in range(4):
                    i = 8 * u + 4 * h + a
                    if i < BS:
                        z = unrotate(v, a)
                        hi = z.astype(BF16)
                        lo = (z - hi.astype(F32)).astype(BF16)
                        a_ref[i * RB : (i + 1) * RB, g * 128 : (g + 1) * 128] = hi
                        a_ref[(BS + i) * RB : (BS + i + 1) * RB, g * 128 : (g + 1) * 128] = lo


def right_panel(r_ref, spread_ref, w_ref, b_ref):
    w_ref[528:552, :] = jnp.zeros((24, 128), F32)
    w_ref[0:NB, :] = r_ref[...].astype(F32)
    pad = jnp.zeros((8, 128), F32)
    full = []
    for a in range(4):
        entries = []
        for q in range(QUADS):
            k = 4 * q + a
            if k < BS:
                entries += [w_ref[pl.ds(k, 24, stride=BS), :], pad]
            else:
                entries += [pad] * 4
        entries = jnp.concatenate(entries, axis=0).astype(BF16)
        full.append(jnp.dot(entries, spread_ref[a], preferred_element_type=F32))
    for q in range(QUADS):
        for g in range(4):
            v = [f[q * JP : q * JP + 24, g * 128 : (g + 1) * 128] for f in full]
            for a in range(4):
                z = jnp.concatenate([unrotate(v, a), pad], axis=0).astype(BF16)
                at = (4 * g + a) * JP
                b_ref[at : at + JP, q * 128 : (q + 1) * 128] = z


def multiply(a_ref, b_ref, p_ref, add_ref=None):
    for u in range(3):
        both = jnp.dot(a_ref[...], b_ref[:, 256 * u : 256 * (u + 1)], preferred_element_type=F32)
        for i in range(BS):
            total = both[i * RB : (i + 1) * RB] + both[(BS + i) * RB : (BS + i + 1) * RB]
            for h in range(2):
                part = total[:, 128 * h : 128 * (h + 1)]
                at = (2 * u + h, pl.ds(i, RB, stride=24), slice(None))
                p_ref[at] = part if add_ref is None else part + add_ref[at]


def first_kernel(counts_hbm, rows_hbm, cols_hbm, kcols_hbm, l_hbm, r_hbm,
                 p_ref, t_ref, pick_ref, spread_ref,
                 counts, rows, cols, kcols, l_ref, r_ref, a_ref, w_ref, b_ref, sems):
    moves = [
        pltpu.make_async_copy(s, d, sems.at[n])
        for n, (s, d) in enumerate((
            (counts_hbm, counts), (rows_hbm, rows), (cols_hbm, cols), (kcols_hbm, kcols),
            (l_hbm, l_ref), (r_hbm, r_ref),
        ))
    ]
    for move in moves:
        move.start()
    spread_matrix(t_ref)
    for move in moves:
        move.wait()
    ncol, nrow = rows.shape[1], kcols.shape[0]
    for s in range(3):
        panel = lax.rem(lax.axis_index("col") + s, ncol)
        source = lax.rem(lax.axis_index("row") + s, nrow)
        pick_ref[s] = slot_pick(rows[0, pl.ds(panel, 1), :], cols[0, pl.ds(panel, 1), :], counts[0, panel])
        for a in range(4):
            spread_ref[s, a] = column_spread(kcols[source], a)
    left_panel(l_ref, pick_ref[0], t_ref, a_ref)
    right_panel(r_ref, spread_ref.at[0], w_ref, b_ref)
    multiply(a_ref, b_ref, p_ref)


def far_left_kernel(l2, t_ref, pick_ref, _, a_ref):
    left_panel(l2, pick_ref[2], t_ref, a_ref)


def far_right_kernel(a_ref, r2, spread_ref, first_ref, p_ref, w_ref, b_ref):
    right_panel(r2, spread_ref.at[2], w_ref, b_ref)
    multiply(a_ref, b_ref, p_ref, first_ref)


def near_right_kernel(r1, spread_ref, _, b_ref, w_ref):
    right_panel(r1, spread_ref.at[1], w_ref, b_ref)


def last_kernel(l1, t_ref, pick_ref, b_ref, before_ref, out_hbm, a_ref, p_ref, h_ref, o_ref, sems):
    left_panel(l1, pick_ref[1], t_ref, a_ref)
    multiply(a_ref, b_ref, p_ref)
    out = out_hbm.reshape(NB * 4, 128)
    moves = []
    for ib in range(3):
        n = 8 if ib < 2 else 7
        for rq in range(RB // 4):
            for q in range(QUADS):
                at = [(4 * rq + a) * 24 + ib * 8 for a in range(4)]
                v = [p_ref[q, t : t + 8, :] + before_ref[q, t : t + 8, :] for t in at]
                half = lanes_like(v[0]) < 64
                for a in (0, 1):
                    h_ref[q, rq, a] = jnp.where(half, v[a], pltpu.roll(v[a + 2], 64, 1))
                    h_ref[q, rq, a + 2] = jnp.where(half, pltpu.roll(v[a], 64, 1), v[a + 2])
        for rq in range(RB // 4):
            for q in range(QUADS):
                for a in (0, 2):
                    x, y = h_ref[q, rq, a], h_ref[q, rq, a + 1]
                    even = (lanes_like(x) & 32) == 0
                    z = (jnp.where(even, x, pltpu.roll(y, 32, 1)), jnp.where(even, pltpu.roll(x, 96, 1), y))
                    for b in range(2):
                        k = 4 * q + a + b
                        if k < BS:
                            o_ref[pl.ds((ib * 8 * BS + k) * 4 + rq, n, stride=4 * BS), :] = z[b][:n]
        part = pl.ds(ib * 8 * BS * 4, n * BS * 4)
        moves.append(pltpu.make_async_copy(o_ref.at[part], out.at[part], sems.at[ib]))
        moves[-1].start()
    for move in moves:
        move.wait()


VMEM = pl.BlockSpec(memory_space=pltpu.VMEM)
ANY = pl.BlockSpec(memory_space=pl.ANY)


def shape(*dims, dtype=F32):
    return jax.ShapeDtypeStruct(dims, dtype)


def call(kernel, flops, out_shape, in_specs, out_specs, scratch):
    return pl.pallas_call(
        kernel,
        out_shape=out_shape,
        in_specs=in_specs,
        out_specs=out_specs,
        scratch_shapes=scratch,
        compiler_params=pltpu.CompilerParams(vmem_limit_bytes=24 * 1024 * 1024),
        cost_estimate=pl.CostEstimate(flops=flops, bytes_accessed=1, transcendentals=0),
    )


def body(left_blocks, left_rows, left_cols, left_counts, right_blocks, right_cols):
    left = left_blocks[0, 0]
    right = jnp.swapaxes(right_blocks[0, 0], 0, 1)
    kcols = jnp.swapaxes(right_cols[:, 0], 1, 2)
    l2, r2 = from_behind(left, "col", -2), from_behind(right, "row", -2)
    r1, l1 = from_behind(right, "row", -1), from_behind(left, "col", -1)
    sums = shape(QUADS, RB * 24, 128)
    dense_left = shape(2 * ROWS, DEPTH, dtype=BF16)
    dense_right = shape(DEPTH, WIDE, dtype=BF16)
    a_scratch = pltpu.VMEM(dense_left.shape, BF16)
    b_scratch = pltpu.VMEM(dense_right.shape, BF16)
    w_scratch = pltpu.VMEM((552, 128), F32)
    first, spread_t, pick, spread = call(
        first_kernel, 1,
        (sums, shape(NB, WIDE, dtype=BF16), shape(3, KB * RB, SA, dtype=BF16), shape(3, 4, KB * BPK, KB * CB, dtype=BF16)),
        [ANY] * 6, (VMEM,) * 4,
        [
            pltpu.SMEM(left_counts.shape, jnp.int32),
            pltpu.VMEM(left_rows.shape, jnp.int32),
            pltpu.VMEM(left_cols.shape, jnp.int32),
            pltpu.VMEM(kcols.shape, jnp.int32),
            pltpu.VMEM((SA, NB), BF16),
            pltpu.VMEM((NB, 128), BF16),
            a_scratch, w_scratch, b_scratch,
            pltpu.SemaphoreType.DMA((6,)),
        ],
    )(*(pltpu.with_memory_space_constraint(x, pltpu.HBM) for x in (left_counts, left_rows, left_cols, kcols, left, right)))
    far_left = call(far_left_kernel, 10**10, dense_left, [VMEM] * 3 + [ANY], VMEM, [])(l2, spread_t, pick, first)
    before = call(
        far_right_kernel, 10**10, sums, [VMEM] * 4, VMEM, [w_scratch, b_scratch],
    )(far_left, r2, spread, first)
    near_right = call(near_right_kernel, 10**10, dense_right, [VMEM] * 2 + [ANY], VMEM, [w_scratch])(r1, spread, before)
    out = call(
        last_kernel, 10**10, shape(NB, 1, RB * CB), [VMEM] * 5, ANY,
        [
            a_scratch,
            pltpu.VMEM(sums.shape, F32),
            pltpu.VMEM((QUADS, 4, 4, 8, 128), F32),
            pltpu.VMEM((2120, 128), F32),
            pltpu.SemaphoreType.DMA((3,)),
        ],
    )(l1, spread_t, pick, near_right, before)
    return jnp.transpose(out[None], (0, 2, 3, 1))


def solution(mesh):
    in_specs = (
        P("row", "col", None, None),
        P("row", None, None),
        P("row", None, None),
        P("row", None),
        P("row", "col", None, None),
        P(None, "col", None, None),
    )
    out_specs = P("row", "col", None, None)
    return jax.shard_map(body, mesh=mesh, in_specs=in_specs, out_specs=out_specs, check_vma=False)
```

```python
import jax
import jax.numpy as jnp
from jax import lax
from jax.experimental import pallas as pl
from jax.experimental.pallas import tpu as pltpu
from jax.sharding import PartitionSpec as P

BS = 23
RB = 16
CB = 32
KB = 16
BPK = 8
SA = 64
JP = 32
QUADS = 6
NB = BS * BS
ROWS = BS * RB
WIDE = QUADS * 128
DEPTH = KB * JP
PAIRS = 12
SPANS = tuple((46 * u // 128 * 128, min(-(-min(46 * u + 46, NB) // 128) * 128, NB)) for u in range(PAIRS))
SPANS = tuple((start, NB if stop > 512 else stop) for start, stop in SPANS)
AT = tuple(sum(stop - start for start, stop in SPANS[:u]) for u in range(PAIRS + 1))
F32 = jnp.float32
BF16 = jnp.bfloat16


def from_behind(value, axis, by):
    devices = lax.axis_size(axis)
    return lax.ppermute(value, axis, [(i, (i + by) % devices) for i in range(devices)])


def lanes_like(v):
    return lax.broadcasted_iota(jnp.int32, v.shape, 1)


def unrotate(v, shift):
    chunk = lanes_like(v[0]) >> 5
    z = v[(3 - shift) % 4]
    for p in range(3):
        z = jnp.where(chunk == p, v[(p - shift) % 4], z)
    return pltpu.roll(z, 128 - 32 * shift, 1) if shift else z


def spread_matrix(t_ref):
    for u, (start, stop) in enumerate(SPANS):
        lane = lax.broadcasted_iota(jnp.int32, (1, 256), 1)
        i, j = 2 * u + (lane >> 7), lane & 31
        source = jnp.where((j < BS) & (i < BS), i * BS + j, -1)
        entry = lax.broadcasted_iota(jnp.int32, (stop - start, 256), 0) + start
        t_ref[AT[u] : AT[u + 1], :] = jnp.where(entry == source, 1.0, 0.0).astype(BF16)


def slot_pick(rows, cols, count):
    slot = lax.broadcasted_iota(jnp.int32, (1, SA), 1)
    code = jnp.where(slot < count, (cols >> 2) * RB + rows, -1)
    place = lax.broadcasted_iota(jnp.int32, (4 * RB, SA), 0)
    return jnp.where(place == code, 1.0, 0.0).astype(BF16)


def slot_mask(cols):
    quarter = lax.broadcasted_iota(jnp.int32, (8, SA), 0)
    mine = jnp.where(quarter == (cols & 3), 1.0, 0.0)
    lane = lax.broadcasted_iota(jnp.int32, (8, 256), 1)
    quarter = lax.broadcasted_iota(jnp.int32, (8, 256), 0)
    chunk = jnp.where(quarter == ((lane >> 5) & 3), 1.0, 0.0)
    return lax.dot_general(mine, chunk, (((0,), (0,)), ((), ())), preferred_element_type=F32).astype(BF16)


def column_spread(cols, spread_ref):
    lane = lax.broadcasted_iota(jnp.int32, (BPK, 128), 1)
    none = jnp.zeros((BPK, 128), F32)
    hits = [(lane & 31) == cols[:, kap : kap + 1] for kap in range(KB)]
    for turn in range(4):
        spread = []
        for kap in range(KB):
            one = jnp.where(hits[kap] & ((lane >> 5) == (kap + turn) % 4), 1.0, 0.0)
            spread.append(jnp.concatenate([one if g == kap // 4 else none for g in range(4)], axis=1))
        spread_ref[turn] = jnp.concatenate(spread, axis=0).astype(BF16)


def left_panel(l_ref, pick, mask, t_ref, a_ref):
    wide = []
    for u, (start, stop) in enumerate(SPANS):
        copies = jnp.dot(l_ref[:, start:stop], t_ref[AT[u] : AT[u + 1], :], preferred_element_type=F32)
        wide.append(copies.astype(BF16) * mask)
    for u in range(PAIRS):
        sums = jnp.dot(pick, wide[u], preferred_element_type=F32)
        hi = sums.astype(BF16)
        lo = (sums - hi.astype(F32)).astype(BF16)
        for h in range(2):
            i = 2 * u + h
            if i < BS:
                for g in range(KB // 4):
                    rows, lanes = slice(g * RB, (g + 1) * RB), slice(h * 128, (h + 1) * 128)
                    a_ref[i * RB : (i + 1) * RB, g * 128 : (g + 1) * 128] = hi[rows, lanes]
                    a_ref[(BS + i) * RB : (BS + i + 1) * RB, g * 128 : (g + 1) * 128] = lo[rows, lanes]


def right_panel(r_ref, spread_ref, w_ref, b_ref):
    w_ref[528:552, :] = jnp.zeros((24, 128), F32)
    w_ref[0:NB, :] = r_ref[...].astype(F32)
    pad = jnp.zeros((8, 128), F32)
    full = []
    for a in range(4):
        entries = []
        for q in range(QUADS):
            k = 4 * q + a
            if k < BS:
                entries += [w_ref[pl.ds(k, 24, stride=BS), :], pad]
            else:
                entries += [pad] * 4
        entries = jnp.concatenate(entries, axis=0).astype(BF16)
        full.append(jnp.dot(entries, spread_ref[a], preferred_element_type=F32))
    for q in range(QUADS):
        for g in range(4):
            v = [f[q * JP : q * JP + 24, g * 128 : (g + 1) * 128] for f in full]
            for a in range(4):
                z = jnp.concatenate([unrotate(v, a), pad], axis=0).astype(BF16)
                at = (4 * g + a) * JP
                b_ref[at : at + JP, q * 128 : (q + 1) * 128] = z


def product(panels, u):
    both = sum(jnp.dot(a[...], b[:, 256 * u : 256 * (u + 1)], preferred_element_type=F32) for a, b in panels)
    return both[:ROWS] + both[ROWS:]


def put_rows(p_ref, add_ref, total, u):
    for i in range(BS):
        for h in range(2):
            part = total[i * RB : (i + 1) * RB, 128 * h : 128 * (h + 1)]
            at = (2 * u + h, pl.ds(i, RB, stride=24), slice(None))
            p_ref[at] = part if add_ref is None else part + add_ref[at]


def first_kernel(counts_hbm, rows_hbm, cols_hbm, kcols_hbm, l_hbm, r_hbm,
                 a_ref, b_ref, r_ref, t_ref, pick_ref, mask_ref, spread_ref,
                 counts, rows, cols, kcols, l_ref, w_ref, sems):
    moves = [
        pltpu.make_async_copy(s, d, sems.at[n])
        for n, (s, d) in enumerate((
            (counts_hbm, counts), (rows_hbm, rows), (cols_hbm, cols), (kcols_hbm, kcols),
            (r_hbm, r_ref), (l_hbm, l_ref),
        ))
    ]
    for move in moves:
        move.start()
    spread_matrix(t_ref)
    for move in moves:
        move.wait()
    ncol, nrow = rows.shape[1], kcols.shape[0]
    for s in range(3):
        panel = lax.rem(lax.axis_index("col") + s, ncol)
        source = lax.rem(lax.axis_index("row") + s, nrow)
        panel_cols = cols[0, pl.ds(panel, 1), :]
        pick_ref[s] = slot_pick(rows[0, pl.ds(panel, 1), :], panel_cols, counts[0, panel])
        mask_ref[s] = slot_mask(panel_cols)
        column_spread(kcols[source], spread_ref.at[s])
    right_panel(r_ref, spread_ref.at[0], w_ref, b_ref)
    left_panel(l_ref, pick_ref[0], mask_ref[0], t_ref, a_ref)


def relay_kernel(r0, r2, _, x_ref):
    odd = lax.rem(lax.axis_index("row"), 2)

    @pl.when(odd == 1)
    def _():
        x_ref[...] = r0[...]

    @pl.when(odd == 0)
    def _():
        x_ref[...] = r2[...]


def far_right_kernel(r, spread_ref, a0, b0, _, b_ref, p_ref, w_ref):
    right_panel(r, spread_ref.at[2], w_ref, b_ref)
    for u in range(3):
        put_rows(p_ref, None, product(((a0, b0),), u), u)


def last_kernel(l2, l1, r1, t_ref, pick_ref, mask_ref, spread_ref, b2, before_ref, out_hbm, a2, a1, b1, w_ref, p_ref, h_ref, o_ref, sems):
    left_panel(l2, pick_ref[2], mask_ref[2], t_ref, a2)
    left_panel(l1, pick_ref[1], mask_ref[1], t_ref, a1)
    right_panel(r1, spread_ref.at[1], w_ref, b1)
    out = out_hbm.reshape(NB * 4, 128)
    moves = []
    for u in range(3):
        put_rows(p_ref, before_ref, product(((a2, b2), (a1, b1)), u), u)
        for part in ((0, 1, 2),) if u < 2 else ((0,), (1,), (2,)):
            places = [(q, rq, ib) for ib in part for q in (2 * u, 2 * u + 1) for rq in range(RB // 4)]
            for q, rq, ib in places:
                at = [(4 * rq + a) * 24 + ib * 8 for a in range(4)]
                v = [p_ref[q, t : t + 8, :] for t in at]
                half = lanes_like(v[0]) < 64
                for a in (0, 1):
                    h_ref[ib, q, rq, a] = jnp.where(half, v[a], pltpu.roll(v[a + 2], 64, 1))
                    h_ref[ib, q, rq, a + 2] = jnp.where(half, pltpu.roll(v[a], 64, 1), v[a + 2])
            for q, rq, ib in places:
                n = 8 if ib < 2 else 7
                for a in (0, 2):
                    x, y = h_ref[ib, q, rq, a], h_ref[ib, q, rq, a + 1]
                    even = (lanes_like(x) & 32) == 0
                    z = (jnp.where(even, x, pltpu.roll(y, 32, 1)), jnp.where(even, pltpu.roll(x, 96, 1), y))
                    for b in range(2):
                        k = 4 * q + a + b
                        if k < BS:
                            o_ref[pl.ds((ib * 8 * BS + k) * 4 + rq, n, stride=4 * BS), :] = z[b][:n]
            if u == 2:
                rows = pl.ds(part[0] * 8 * BS * 4, (8 if part[0] < 2 else 7) * BS * 4)
                moves.append(pltpu.make_async_copy(o_ref.at[rows], out.at[rows], sems.at[part[0]]))
                moves[-1].start()
    for move in moves:
        move.wait()


VMEM = pl.BlockSpec(memory_space=pltpu.VMEM)
ANY = pl.BlockSpec(memory_space=pl.ANY)


def shape(*dims, dtype=F32):
    return jax.ShapeDtypeStruct(dims, dtype)


def call(kernel, flops, out_shape, in_specs, out_specs, scratch):
    return pl.pallas_call(
        kernel,
        out_shape=out_shape,
        in_specs=in_specs,
        out_specs=out_specs,
        scratch_shapes=scratch,
        compiler_params=pltpu.CompilerParams(vmem_limit_bytes=24 * 1024 * 1024),
        cost_estimate=pl.CostEstimate(flops=flops, bytes_accessed=1, transcendentals=0),
    )


def body(left_blocks, left_rows, left_cols, left_counts, right_blocks, right_cols):
    left = left_blocks[0, 0]
    right = jnp.swapaxes(right_blocks[0, 0], 0, 1)
    kcols = jnp.swapaxes(right_cols[:, 0], 1, 2)
    l2, l1 = from_behind(left, "col", -2), from_behind(left, "col", -1)
    r2 = from_behind(right, "row", -2)
    sums = shape(QUADS, RB * 24, 128)
    dense_left = shape(2 * ROWS, DEPTH, dtype=BF16)
    dense_right = shape(DEPTH, WIDE, dtype=BF16)
    w_scratch = pltpu.VMEM((552, 128), F32)
    a0, b0, r0, spread_t, pick, mask, spread = call(
        first_kernel, 1,
        (
            dense_left, dense_right, shape(NB, 128, dtype=BF16), shape(AT[-1], 256, dtype=BF16),
            shape(3, 4 * RB, SA, dtype=BF16), shape(3, SA, 256, dtype=BF16), shape(3, 4, KB * BPK, KB * CB, dtype=BF16),
        ),
        [ANY] * 6, (VMEM,) * 7,
        [
            pltpu.SMEM(left_counts.shape, jnp.int32),
            pltpu.VMEM(left_rows.shape, jnp.int32),
            pltpu.VMEM(left_cols.shape, jnp.int32),
            pltpu.VMEM(kcols.shape, jnp.int32),
            pltpu.VMEM((SA, NB), BF16),
            w_scratch,
            pltpu.SemaphoreType.DMA((6,)),
        ],
    )(*(pltpu.with_memory_space_constraint(x, pltpu.HBM) for x in (left_counts, left_rows, left_cols, kcols, left, right)))
    relay = call(relay_kernel, 10**10, shape(NB, 128, dtype=BF16), [VMEM] * 2 + [ANY], VMEM, [])(r0, r2, a0)
    r1 = lax.ppermute(relay, "row", [(i, i ^ 1) for i in range(lax.axis_size("row"))])
    b2, before = call(
        far_right_kernel, 10**10, (dense_right, sums), [VMEM] * 4 + [ANY], (VMEM,) * 2, [w_scratch],
    )(r2, spread, a0, b0, relay)
    out = call(
        last_kernel, 10**10, shape(NB, 1, RB * CB), [VMEM] * 9, ANY,
        [
            pltpu.VMEM(dense_left.shape, BF16),
            pltpu.VMEM(dense_left.shape, BF16),
            pltpu.VMEM(dense_right.shape, BF16),
            w_scratch,
            pltpu.VMEM(sums.shape, F32),
            pltpu.VMEM((3, QUADS, 4, 4, 8, 128), F32),
            pltpu.VMEM((2120, 128), F32),
            pltpu.SemaphoreType.DMA((3,)),
        ],
    )(l2, l1, r1, spread_t, pick, mask, spread, b2, before)
    return jnp.transpose(out[None], (0, 2, 3, 1))


def solution(mesh):
    in_specs = (
        P("row", "col", None, None),
        P("row", None, None),
        P("row", None, None),
        P("row", None),
        P("row", "col", None, None),
        P(None, "col", None, None),
    )
    out_specs = P("row", "col", None, None)
    return jax.shard_map(body, mesh=mesh, in_specs=in_specs, out_specs=out_specs, check_vma=False)
```

```python
import jax
import jax.numpy as jnp
from jax import lax
from jax.experimental import pallas as pl
from jax.experimental.pallas import tpu as pltpu
from jax.sharding import PartitionSpec as P

BS = 23
RB = 16
CB = 32
KB = 16
BPK = 8
SA = 64
JP = 32
QUADS = 6
NB = BS * BS
ROWS = BS * RB
WIDE = QUADS * 128
DEPTH = KB * JP
PAIRS = 12
SPANS = tuple((46 * u // 128 * 128, min(-(-min(46 * u + 46, NB) // 128) * 128, NB)) for u in range(PAIRS))
SPANS = tuple((start, NB if stop > 512 else stop) for start, stop in SPANS)
AT = tuple(sum(stop - start for start, stop in SPANS[:u]) for u in range(PAIRS + 1))
F32 = jnp.float32
BF16 = jnp.bfloat16


def from_behind(value, axis, by):
    devices = lax.axis_size(axis)
    return lax.ppermute(value, axis, [(i, (i + by) % devices) for i in range(devices)])


def lanes_like(v):
    return lax.broadcasted_iota(jnp.int32, v.shape, 1)


def unrotate(v, shift):
    chunk = lanes_like(v[0]) >> 5
    z = v[(3 - shift) % 4]
    for p in range(3):
        z = jnp.where(chunk == p, v[(p - shift) % 4], z)
    return pltpu.roll(z, 128 - 32 * shift, 1) if shift else z


def spread_matrix(t_ref):
    for u, (start, stop) in enumerate(SPANS):
        lane = lax.broadcasted_iota(jnp.int32, (1, 256), 1)
        i, j = 2 * u + (lane >> 7), lane & 31
        source = jnp.where((j < BS) & (i < BS), i * BS + j, -1)
        entry = lax.broadcasted_iota(jnp.int32, (stop - start, 256), 0) + start
        t_ref[AT[u] : AT[u + 1], :] = jnp.where(entry == source, 1.0, 0.0).astype(BF16)


def slot_pick(rows, cols, count):
    slot = lax.broadcasted_iota(jnp.int32, (1, SA), 1)
    code = jnp.where(slot < count, (cols >> 2) * RB + rows, -1)
    place = lax.broadcasted_iota(jnp.int32, (4 * RB, SA), 0)
    return jnp.where(place == code, 1.0, 0.0).astype(BF16)


def slot_mask(cols):
    quarter = lax.broadcasted_iota(jnp.int32, (8, SA), 0)
    mine = jnp.where(quarter == (cols & 3), 1.0, 0.0)
    lane = lax.broadcasted_iota(jnp.int32, (8, 256), 1)
    quarter = lax.broadcasted_iota(jnp.int32, (8, 256), 0)
    chunk = jnp.where(quarter == ((lane >> 5) & 3), 1.0, 0.0)
    return lax.dot_general(mine, chunk, (((0,), (0,)), ((), ())), preferred_element_type=F32).astype(BF16)


def column_spread(cols, spread_ref):
    lane = lax.broadcasted_iota(jnp.int32, (BPK, 128), 1)
    none = jnp.zeros((BPK, 128), F32)
    hits = [(lane & 31) == cols[:, kap : kap + 1] for kap in range(KB)]
    for turn in range(4):
        spread = []
        for kap in range(KB):
            one = jnp.where(hits[kap] & ((lane >> 5) == (kap + turn) % 4), 1.0, 0.0)
            spread.append(jnp.concatenate([one if g == kap // 4 else none for g in range(4)], axis=1))
        spread_ref[turn] = jnp.concatenate(spread, axis=0).astype(BF16)


def left_panel(l_ref, pick, mask, t_ref, a_ref):
    wide = []
    for u, (start, stop) in enumerate(SPANS):
        copies = jnp.dot(l_ref[:, start:stop], t_ref[AT[u] : AT[u + 1], :], preferred_element_type=F32)
        wide.append(copies.astype(BF16) * mask)
    for u in range(PAIRS):
        sums = jnp.dot(pick, wide[u], preferred_element_type=F32)
        hi = sums.astype(BF16)
        lo = (sums - hi.astype(F32)).astype(BF16)
        for h in range(2):
            i = 2 * u + h
            if i < BS:
                for g in range(KB // 4):
                    rows, lanes = slice(g * RB, (g + 1) * RB), slice(h * 128, (h + 1) * 128)
                    a_ref[i * RB : (i + 1) * RB, g * 128 : (g + 1) * 128] = hi[rows, lanes]
                    a_ref[i * RB : (i + 1) * RB, DEPTH + g * 128 : DEPTH + (g + 1) * 128] = lo[rows, lanes]


def right_panel(r_ref, spread_ref, w_ref, b_ref):
    w_ref[528:552, :] = jnp.zeros((24, 128), F32)
    w_ref[0:NB, :] = r_ref[...].astype(F32)
    pad = jnp.zeros((8, 128), F32)
    full = []
    for a in range(4):
        entries = []
        for q in range(QUADS):
            k = 4 * q + a
            if k < BS:
                entries += [w_ref[pl.ds(k, 24, stride=BS), :], pad]
            else:
                entries += [pad] * 4
        entries = jnp.concatenate(entries, axis=0).astype(BF16)
        full.append(jnp.dot(entries, spread_ref[a], preferred_element_type=F32))
    for q in range(QUADS):
        for g in range(4):
            v = [f[q * JP : q * JP + 24, g * 128 : (g + 1) * 128] for f in full]
            for a in range(4):
                z = jnp.concatenate([unrotate(v, a), pad], axis=0).astype(BF16)
                at = (4 * g + a) * JP
                b_ref[at : at + JP, q * 128 : (q + 1) * 128] = z


def product(panels, u):
    total = None
    for a, b in panels:
        for part in range(2):
            one = jnp.dot(a[:, part * DEPTH : (part + 1) * DEPTH], b[:, 256 * u : 256 * (u + 1)], preferred_element_type=F32)
            total = one if total is None else total + one
    return total


def put_rows(p_ref, add_ref, total, u):
    for i in range(BS):
        for h in range(2):
            part = total[i * RB : (i + 1) * RB, 128 * h : 128 * (h + 1)]
            at = (2 * u + h, pl.ds(i, RB, stride=24), slice(None))
            p_ref[at] = part if add_ref is None else part + add_ref[at]


def first_kernel(counts_hbm, rows_hbm, cols_hbm, kcols_hbm, l_hbm, r_hbm,
                 a_ref, b_ref, r_ref, t_ref, pick_ref, mask_ref, spread_ref,
                 counts, rows, cols, kcols, l_ref, w_ref, sems):
    moves = [
        pltpu.make_async_copy(s, d, sems.at[n])
        for n, (s, d) in enumerate((
            (counts_hbm, counts), (rows_hbm, rows), (cols_hbm, cols), (kcols_hbm, kcols),
            (r_hbm, r_ref), (l_hbm, l_ref),
        ))
    ]
    for move in moves:
        move.start()
    spread_matrix(t_ref)
    for move in moves:
        move.wait()
    ncol, nrow = rows.shape[1], kcols.shape[0]
    for s in range(3):
        panel = lax.rem(lax.axis_index("col") + s, ncol)
        source = lax.rem(lax.axis_index("row") + s, nrow)
        panel_cols = cols[0, pl.ds(panel, 1), :]
        pick_ref[s] = slot_pick(rows[0, pl.ds(panel, 1), :], panel_cols, counts[0, panel])
        mask_ref[s] = slot_mask(panel_cols)
        column_spread(kcols[source], spread_ref.at[s])
    right_panel(r_ref, spread_ref.at[0], w_ref, b_ref)
    left_panel(l_ref, pick_ref[0], mask_ref[0], t_ref, a_ref)


def relay_kernel(r0, r2, _, x_ref):
    odd = lax.rem(lax.axis_index("row"), 2)

    @pl.when(odd == 1)
    def _():
        x_ref[...] = r0[...]

    @pl.when(odd == 0)
    def _():
        x_ref[...] = r2[...]


def far_right_kernel(r, spread_ref, a0, b0, _, b_ref, p_ref, w_ref):
    right_panel(r, spread_ref.at[2], w_ref, b_ref)
    for u in range(3):
        put_rows(p_ref, None, product(((a0, b0),), u), u)


def last_kernel(l2, l1, r1, t_ref, pick_ref, mask_ref, spread_ref, b2, before_ref, out_hbm, a2, a1, b1, w_ref, p_ref, h_ref, o_ref, sems):
    left_panel(l2, pick_ref[2], mask_ref[2], t_ref, a2)
    left_panel(l1, pick_ref[1], mask_ref[1], t_ref, a1)
    right_panel(r1, spread_ref.at[1], w_ref, b1)
    out = out_hbm.reshape(NB * 4, 128)
    moves = []
    for u in range(3):
        put_rows(p_ref, before_ref, product(((a2, b2), (a1, b1)), u), u)
        for part in ((0, 1, 2),) if u < 2 else ((0,), (1,), (2,)):
            places = [(q, rq, ib) for ib in part for q in (2 * u, 2 * u + 1) for rq in range(RB // 4)]
            for q, rq, ib in places:
                at = [(4 * rq + a) * 24 + ib * 8 for a in range(4)]
                v = [p_ref[q, t : t + 8, :] for t in at]
                half = lanes_like(v[0]) < 64
                for a in (0, 1):
                    h_ref[ib, q, rq, a] = jnp.where(half, v[a], pltpu.roll(v[a + 2], 64, 1))
                    h_ref[ib, q, rq, a + 2] = jnp.where(half, pltpu.roll(v[a], 64, 1), v[a + 2])
            for q, rq, ib in places:
                n = 8 if ib < 2 else 7
                for a in (0, 2):
                    x, y = h_ref[ib, q, rq, a], h_ref[ib, q, rq, a + 1]
                    even = (lanes_like(x) & 32) == 0
                    z = (jnp.where(even, x, pltpu.roll(y, 32, 1)), jnp.where(even, pltpu.roll(x, 96, 1), y))
                    for b in range(2):
                        k = 4 * q + a + b
                        if k < BS:
                            o_ref[pl.ds((ib * 8 * BS + k) * 4 + rq, n, stride=4 * BS), :] = z[b][:n]
            if u == 2:
                rows = pl.ds(part[0] * 8 * BS * 4, (8 if part[0] < 2 else 7) * BS * 4)
                moves.append(pltpu.make_async_copy(o_ref.at[rows], out.at[rows], sems.at[part[0]]))
                moves[-1].start()
    for move in moves:
        move.wait()


VMEM = pl.BlockSpec(memory_space=pltpu.VMEM)
ANY = pl.BlockSpec(memory_space=pl.ANY)


def shape(*dims, dtype=F32):
    return jax.ShapeDtypeStruct(dims, dtype)


def call(kernel, flops, out_shape, in_specs, out_specs, scratch):
    return pl.pallas_call(
        kernel,
        out_shape=out_shape,
        in_specs=in_specs,
        out_specs=out_specs,
        scratch_shapes=scratch,
        compiler_params=pltpu.CompilerParams(vmem_limit_bytes=24 * 1024 * 1024),
        cost_estimate=pl.CostEstimate(flops=flops, bytes_accessed=1, transcendentals=0),
    )


def body(left_blocks, left_rows, left_cols, left_counts, right_blocks, right_cols):
    left = left_blocks[0, 0]
    right = jnp.swapaxes(right_blocks[0, 0], 0, 1)
    kcols = jnp.swapaxes(right_cols[:, 0], 1, 2)
    l2, l1 = from_behind(left, "col", -2), from_behind(left, "col", -1)
    r2 = from_behind(right, "row", -2)
    sums = shape(QUADS, RB * 24, 128)
    dense_left = shape(ROWS, 2 * DEPTH, dtype=BF16)
    dense_right = shape(DEPTH, WIDE, dtype=BF16)
    w_scratch = pltpu.VMEM((552, 128), F32)
    a0, b0, r0, spread_t, pick, mask, spread = call(
        first_kernel, 1,
        (
            dense_left, dense_right, shape(NB, 128, dtype=BF16), shape(AT[-1], 256, dtype=BF16),
            shape(3, 4 * RB, SA, dtype=BF16), shape(3, SA, 256, dtype=BF16), shape(3, 4, KB * BPK, KB * CB, dtype=BF16),
        ),
        [ANY] * 6, (VMEM,) * 7,
        [
            pltpu.SMEM(left_counts.shape, jnp.int32),
            pltpu.VMEM(left_rows.shape, jnp.int32),
            pltpu.VMEM(left_cols.shape, jnp.int32),
            pltpu.VMEM(kcols.shape, jnp.int32),
            pltpu.VMEM((SA, NB), BF16),
            w_scratch,
            pltpu.SemaphoreType.DMA((6,)),
        ],
    )(*(pltpu.with_memory_space_constraint(x, pltpu.HBM) for x in (left_counts, left_rows, left_cols, kcols, left, right)))
    relay = call(relay_kernel, 10**10, shape(NB, 128, dtype=BF16), [VMEM] * 2 + [ANY], VMEM, [])(r0, r2, a0)
    r1 = lax.ppermute(relay, "row", [(i, i ^ 1) for i in range(lax.axis_size("row"))])
    b2, before = call(
        far_right_kernel, 10**10, (dense_right, sums), [VMEM] * 4 + [ANY], (VMEM,) * 2, [w_scratch],
    )(r2, spread, a0, b0, relay)
    out = call(
        last_kernel, 10**10, shape(NB, 1, RB * CB), [VMEM] * 9, ANY,
        [
            pltpu.VMEM(dense_left.shape, BF16),
            pltpu.VMEM(dense_left.shape, BF16),
            pltpu.VMEM(dense_right.shape, BF16),
            w_scratch,
            pltpu.VMEM(sums.shape, F32),
            pltpu.VMEM((3, QUADS, 4, 4, 8, 128), F32),
            pltpu.VMEM((2120, 128), F32),
            pltpu.SemaphoreType.DMA((3,)),
        ],
    )(l2, l1, r1, spread_t, pick, mask, spread, b2, before)
    return jnp.transpose(out[None], (0, 2, 3, 1))


def solution(mesh):
    in_specs = (
        P("row", "col", None, None),
        P("row", None, None),
        P("row", None, None),
        P("row", None),
        P("row", "col", None, None),
        P(None, "col", None, None),
    )
    out_specs = P("row", "col", None, None)
    return jax.shard_map(body, mesh=mesh, in_specs=in_specs, out_specs=out_specs, check_vma=False)
```

```python
import jax
import jax.numpy as jnp
from jax import lax
from jax.experimental import pallas as pl
from jax.experimental.pallas import tpu as pltpu
from jax.sharding import PartitionSpec as P

BS = 23
RB = 16
CB = 32
KB = 16
BPK = 8
SA = 64
JP = 32
QUADS = 6
NB = BS * BS
ROWS = BS * RB
WIDE = QUADS * 128
DEPTH = KB * JP
PAIRS = 12
SPANS = tuple((46 * u // 128 * 128, min(-(-min(46 * u + 46, NB) // 128) * 128, NB)) for u in range(PAIRS))
SPANS = tuple((start, NB if stop > 512 else stop) for start, stop in SPANS)
AT = tuple(sum(stop - start for start, stop in SPANS[:u]) for u in range(PAIRS + 1))
F32 = jnp.float32
BF16 = jnp.bfloat16


def from_behind(value, axis, by):
    devices = lax.axis_size(axis)
    return lax.ppermute(value, axis, [(i, (i + by) % devices) for i in range(devices)])


def lanes_like(v):
    return lax.broadcasted_iota(jnp.int32, v.shape, 1)


def unrotate(v, shift):
    chunk = lanes_like(v[0]) >> 5
    z = v[(3 - shift) % 4]
    for p in range(3):
        z = jnp.where(chunk == p, v[(p - shift) % 4], z)
    return pltpu.roll(z, 128 - 32 * shift, 1) if shift else z


def spread_matrix(t_ref):
    for u, (start, stop) in enumerate(SPANS):
        lane = lax.broadcasted_iota(jnp.int32, (1, 256), 1)
        i, j = 2 * u + (lane >> 7), lane & 31
        source = jnp.where((j < BS) & (i < BS), i * BS + j, -1)
        entry = lax.broadcasted_iota(jnp.int32, (stop - start, 256), 0) + start
        t_ref[AT[u] : AT[u + 1], :] = jnp.where(entry == source, 1.0, 0.0).astype(BF16)


def slot_code(rows, cols, count):
    slot = lax.broadcasted_iota(jnp.int32, (1, SA), 1)
    return jnp.where(slot < count, (cols >> 2) * RB + rows, -1)


def slot_pick(code):
    place = lax.broadcasted_iota(jnp.int32, (4 * RB, SA), 0)
    return jnp.where(place == code, 1.0, 0.0).astype(BF16)


def slot_mask(cols):
    quarter = lax.broadcasted_iota(jnp.int32, (8, SA), 0)
    mine = jnp.where(quarter == (cols & 3), 1.0, 0.0)
    lane = lax.broadcasted_iota(jnp.int32, (8, 256), 1)
    quarter = lax.broadcasted_iota(jnp.int32, (8, 256), 0)
    chunk = jnp.where(quarter == ((lane >> 5) & 3), 1.0, 0.0)
    return lax.dot_general(mine, chunk, (((0,), (0,)), ((), ())), preferred_element_type=F32).astype(BF16)


def column_spread(cols, spread_ref):
    lane = lax.broadcasted_iota(jnp.int32, (BPK, 128), 1)
    none = jnp.zeros((BPK, 128), F32)
    hits = [(lane & 31) == cols[:, kap : kap + 1] for kap in range(KB)]
    for turn in range(4):
        spread = []
        for kap in range(KB):
            one = jnp.where(hits[kap] & ((lane >> 5) == (kap + turn) % 4), 1.0, 0.0)
            spread.append(jnp.concatenate([one if g == kap // 4 else none for g in range(4)], axis=1))
        spread_ref[turn] = jnp.concatenate(spread, axis=0).astype(BF16)


def left_panel(l_ref, slots_ref, s, t_ref, a_ref):
    pick = slot_pick(slots_ref[s : s + 1])
    mask = slot_mask(slots_ref[s + 3 : s + 4])
    wide = []
    for u, (start, stop) in enumerate(SPANS):
        copies = jnp.dot(l_ref[:, start:stop], t_ref[AT[u] : AT[u + 1], :], preferred_element_type=F32)
        wide.append(copies.astype(BF16) * mask)
    for u in range(PAIRS):
        sums = jnp.dot(pick, wide[u], preferred_element_type=F32)
        hi = sums.astype(BF16)
        lo = (sums - hi.astype(F32)).astype(BF16)
        for h in range(2):
            i = 2 * u + h
            if i < BS:
                for g in range(KB // 4):
                    rows, lanes = slice(g * RB, (g + 1) * RB), slice(h * 128, (h + 1) * 128)
                    a_ref[i * RB : (i + 1) * RB, g * 128 : (g + 1) * 128] = hi[rows, lanes]
                    a_ref[i * RB : (i + 1) * RB, DEPTH + g * 128 : DEPTH + (g + 1) * 128] = lo[rows, lanes]


def right_panel(r_ref, spread_ref, w_ref, b_ref):
    w_ref[528:552, :] = jnp.zeros((24, 128), F32)
    w_ref[0:NB, :] = r_ref[...].astype(F32)
    pad = jnp.zeros((8, 128), F32)
    full = []
    for a in range(4):
        entries = []
        for q in range(QUADS):
            k = 4 * q + a
            if k < BS:
                entries += [w_ref[pl.ds(k, 24, stride=BS), :], pad]
            else:
                entries += [pad] * 4
        entries = jnp.concatenate(entries, axis=0).astype(BF16)
        full.append(jnp.dot(entries, spread_ref[a], preferred_element_type=F32))
    for q in range(QUADS):
        for g in range(4):
            v = [f[q * JP : q * JP + 24, g * 128 : (g + 1) * 128] for f in full]
            for a in range(4):
                z = jnp.concatenate([unrotate(v, a), pad], axis=0).astype(BF16)
                at = (4 * g + a) * JP
                b_ref[at : at + JP, q * 128 : (q + 1) * 128] = z


def product(panels, u):
    total = None
    for a, b in panels:
        for part in range(2):
            one = jnp.dot(a[:, part * DEPTH : (part + 1) * DEPTH], b[:, 256 * u : 256 * (u + 1)], preferred_element_type=F32)
            total = one if total is None else total + one
    return total


def put_rows(p_ref, add_ref, total, u):
    for i in range(BS):
        for h in range(2):
            part = total[i * RB : (i + 1) * RB, 128 * h : 128 * (h + 1)]
            at = (2 * u + h, pl.ds(i, RB, stride=24), slice(None))
            p_ref[at] = part if add_ref is None else part + add_ref[at]


def first_kernel(counts_hbm, rows_hbm, cols_hbm, kcols_hbm, l_hbm, r_hbm,
                 a_ref, b_ref, r_ref, t_ref, slots_ref, near_ref,
                 counts, rows, cols, kcols, l_ref, w_ref, spread_ref, sems):
    moves = [
        pltpu.make_async_copy(s, d, sems.at[n])
        for n, (s, d) in enumerate((
            (counts_hbm, counts), (rows_hbm, rows), (cols_hbm, cols), (kcols_hbm, kcols),
            (r_hbm, r_ref), (l_hbm, l_ref),
        ))
    ]
    for move in moves:
        move.start()
    spread_matrix(t_ref)
    for move in moves:
        move.wait()
    ncol, nrow = rows.shape[1], kcols.shape[0]
    for s in range(3):
        panel = lax.rem(lax.axis_index("col") + s, ncol)
        source = lax.rem(lax.axis_index("row") + s, nrow)
        panel_cols = cols[0, pl.ds(panel, 1), :]
        slots_ref[s : s + 1] = slot_code(rows[0, pl.ds(panel, 1), :], panel_cols, counts[0, panel])
        slots_ref[s + 3 : s + 4] = panel_cols
        near_ref[s] = kcols[source]
    column_spread(near_ref[0], spread_ref)
    right_panel(r_ref, spread_ref, w_ref, b_ref)
    left_panel(l_ref, slots_ref, 0, t_ref, a_ref)


def relay_kernel(r0, r2, _, x_ref):
    odd = lax.rem(lax.axis_index("row"), 2)

    @pl.when(odd == 1)
    def _():
        x_ref[...] = r0[...]

    @pl.when(odd == 0)
    def _():
        x_ref[...] = r2[...]


def far_right_kernel(r, near_ref, a0, b0, _, b_ref, p_ref, w_ref, spread_ref):
    column_spread(near_ref[2], spread_ref)
    right_panel(r, spread_ref, w_ref, b_ref)
    for u in range(3):
        put_rows(p_ref, None, product(((a0, b0),), u), u)


def last_kernel(l2, l1, r1, t_ref, slots_ref, near_ref, b2, before_ref, out_hbm, a2, a1, b1, w_ref, spread_ref, p_ref, h_ref, o_ref, sems):
    left_panel(l2, slots_ref, 2, t_ref, a2)
    left_panel(l1, slots_ref, 1, t_ref, a1)
    column_spread(near_ref[1], spread_ref)
    right_panel(r1, spread_ref, w_ref, b1)
    out = out_hbm.reshape(NB * 4, 128)
    moves = []
    for u in range(3):
        put_rows(p_ref, before_ref, product(((a2, b2), (a1, b1)), u), u)
        for part in ((0, 1, 2),) if u < 2 else ((0,), (1,), (2,)):
            places = [(q, rq, ib) for ib in part for q in (2 * u, 2 * u + 1) for rq in range(RB // 4)]
            for q, rq, ib in places:
                at = [(4 * rq + a) * 24 + ib * 8 for a in range(4)]
                v = [p_ref[q, t : t + 8, :] for t in at]
                half = lanes_like(v[0]) < 64
                for a in (0, 1):
                    crossed = pltpu.roll(jnp.where(half, v[a + 2], v[a]), 64, 1)
                    h_ref[ib, q, rq, a] = jnp.where(half, v[a], crossed)
                    h_ref[ib, q, rq, a + 2] = jnp.where(half, crossed, v[a + 2])
            for q, rq, ib in places:
                n = 8 if ib < 2 else 7
                for a in (0, 2):
                    x, y = h_ref[ib, q, rq, a], h_ref[ib, q, rq, a + 1]
                    even = (lanes_like(x) & 32) == 0
                    z = (jnp.where(even, x, pltpu.roll(y, 32, 1)), jnp.where(even, pltpu.roll(x, 96, 1), y))
                    for b in range(2):
                        k = 4 * q + a + b
                        if k < BS:
                            o_ref[pl.ds((ib * 8 * BS + k) * 4 + rq, n, stride=4 * BS), :] = z[b][:n]
            if u == 2:
                rows = pl.ds(part[0] * 8 * BS * 4, (8 if part[0] < 2 else 7) * BS * 4)
                moves.append(pltpu.make_async_copy(o_ref.at[rows], out.at[rows], sems.at[part[0]]))
                moves[-1].start()
    for move in moves:
        move.wait()


VMEM = pl.BlockSpec(memory_space=pltpu.VMEM)
ANY = pl.BlockSpec(memory_space=pl.ANY)


def shape(*dims, dtype=F32):
    return jax.ShapeDtypeStruct(dims, dtype)


def call(kernel, flops, out_shape, in_specs, out_specs, scratch):
    return pl.pallas_call(
        kernel,
        out_shape=out_shape,
        in_specs=in_specs,
        out_specs=out_specs,
        scratch_shapes=scratch,
        compiler_params=pltpu.CompilerParams(vmem_limit_bytes=24 * 1024 * 1024),
        cost_estimate=pl.CostEstimate(flops=flops, bytes_accessed=1, transcendentals=0),
    )


def body(left_blocks, left_rows, left_cols, left_counts, right_blocks, right_cols):
    left = left_blocks[0, 0]
    right = jnp.swapaxes(right_blocks[0, 0], 0, 1)
    kcols = jnp.swapaxes(right_cols[:, 0], 1, 2)
    l2, l1 = from_behind(left, "col", -2), from_behind(left, "col", -1)
    r2 = from_behind(right, "row", -2)
    sums = shape(QUADS, RB * 24, 128)
    dense_left = shape(ROWS, 2 * DEPTH, dtype=BF16)
    dense_right = shape(DEPTH, WIDE, dtype=BF16)
    w_scratch = pltpu.VMEM((552, 128), F32)
    spread_scratch = pltpu.VMEM((4, KB * BPK, KB * CB), BF16)
    a0, b0, r0, spread_t, slots, near = call(
        first_kernel, 1,
        (
            dense_left, dense_right, shape(NB, 128, dtype=BF16), shape(AT[-1], 256, dtype=BF16),
            shape(8, SA, dtype=jnp.int32), shape(3, BPK, KB, dtype=jnp.int32),
        ),
        [ANY] * 6, (VMEM,) * 6,
        [
            pltpu.SMEM(left_counts.shape, jnp.int32),
            pltpu.VMEM(left_rows.shape, jnp.int32),
            pltpu.VMEM(left_cols.shape, jnp.int32),
            pltpu.VMEM(kcols.shape, jnp.int32),
            pltpu.VMEM((SA, NB), BF16),
            w_scratch, spread_scratch,
            pltpu.SemaphoreType.DMA((6,)),
        ],
    )(*(pltpu.with_memory_space_constraint(x, pltpu.HBM) for x in (left_counts, left_rows, left_cols, kcols, left, right)))
    relay = call(relay_kernel, 10**10, shape(NB, 128, dtype=BF16), [VMEM] * 2 + [ANY], VMEM, [])(r0, r2, a0)
    r1 = lax.ppermute(relay, "row", [(i, i ^ 1) for i in range(lax.axis_size("row"))])
    b2, before = call(
        far_right_kernel, 10**10, (dense_right, sums), [VMEM] * 4 + [ANY], (VMEM,) * 2, [w_scratch, spread_scratch],
    )(r2, near, a0, b0, relay)
    out = call(
        last_kernel, 10**10, shape(NB, 1, RB * CB), [VMEM] * 8, ANY,
        [
            pltpu.VMEM(dense_left.shape, BF16),
            pltpu.VMEM(dense_left.shape, BF16),
            pltpu.VMEM(dense_right.shape, BF16),
            w_scratch, spread_scratch,
            pltpu.VMEM(sums.shape, F32),
            pltpu.VMEM((3, QUADS, 4, 4, 8, 128), F32),
            pltpu.VMEM((2120, 128), F32),
            pltpu.SemaphoreType.DMA((3,)),
        ],
    )(l2, l1, r1, spread_t, slots, near, b2, before)
    return jnp.transpose(out[None], (0, 2, 3, 1))


def solution(mesh):
    in_specs = (
        P("row", "col", None, None),
        P("row", None, None),
        P("row", None, None),
        P("row", None),
        P("row", "col", None, None),
        P(None, "col", None, None),
    )
    out_specs = P("row", "col", None, None)
    return jax.shard_map(body, mesh=mesh, in_specs=in_specs, out_specs=out_specs, check_vma=False)
```

```python
import jax
import jax.numpy as jnp
from jax import lax
from jax.experimental import pallas as pl
from jax.experimental.pallas import tpu as pltpu
from jax.sharding import PartitionSpec as P

BS = 23
RB = 16
CB = 32
KB = 16
BPK = 8
SA = 64
JP = 32
QUADS = 6
NB = BS * BS
ROWS = BS * RB
WIDE = QUADS * 128
DEPTH = KB * JP
PAIRS = 12
SPANS = tuple((46 * u // 128 * 128, min(-(-min(46 * u + 46, NB) // 128) * 128, NB)) for u in range(PAIRS))
SPANS = tuple((start, NB if stop > 512 else stop) for start, stop in SPANS)
AT = tuple(sum(stop - start for start, stop in SPANS[:u]) for u in range(PAIRS + 1))
F32 = jnp.float32
BF16 = jnp.bfloat16


def from_behind(value, axis, by):
    devices = lax.axis_size(axis)
    return lax.ppermute(value, axis, [(i, (i + by) % devices) for i in range(devices)])


def lanes_like(v):
    return lax.broadcasted_iota(jnp.int32, v.shape, 1)


def unrotate(v, shift):
    chunk = lanes_like(v[0]) >> 5
    z = v[(3 - shift) % 4]
    for p in range(3):
        z = jnp.where(chunk == p, v[(p - shift) % 4], z)
    return pltpu.roll(z, 128 - 32 * shift, 1) if shift else z


def spread_matrix(t_ref):
    for u, (start, stop) in enumerate(SPANS):
        lane = lax.broadcasted_iota(jnp.int32, (1, 256), 1)
        i, j = 2 * u + (lane >> 7), lane & 31
        source = jnp.where((j < BS) & (i < BS), i * BS + j, -1)
        entry = lax.broadcasted_iota(jnp.int32, (stop - start, 256), 0) + start
        t_ref[AT[u] : AT[u + 1], :] = jnp.where(entry == source, 1.0, 0.0).astype(BF16)


def slot_code(rows, cols, count):
    slot = lax.broadcasted_iota(jnp.int32, (1, SA), 1)
    return jnp.where(slot < count, (cols >> 2) * RB + rows, -1)


def slot_pick(code):
    place = lax.broadcasted_iota(jnp.int32, (4 * RB, SA), 0)
    return jnp.where(place == code, 1.0, 0.0).astype(BF16)


def slot_mask(cols):
    quarter = lax.broadcasted_iota(jnp.int32, (8, SA), 0)
    mine = jnp.where(quarter == (cols & 3), 1.0, 0.0)
    lane = lax.broadcasted_iota(jnp.int32, (8, 256), 1)
    quarter = lax.broadcasted_iota(jnp.int32, (8, 256), 0)
    chunk = jnp.where(quarter == ((lane >> 5) & 3), 1.0, 0.0)
    return lax.dot_general(mine, chunk, (((0,), (0,)), ((), ())), preferred_element_type=F32).astype(BF16)


def column_spread(cols, spread_ref):
    lane = lax.broadcasted_iota(jnp.int32, (BPK, 128), 1)
    none = jnp.zeros((BPK, 128), F32)
    hits = [(lane & 31) == cols[:, kap : kap + 1] for kap in range(KB)]
    for turn in range(4):
        spread = []
        for kap in range(KB):
            one = jnp.where(hits[kap] & ((lane >> 5) == (kap + turn) % 4), 1.0, 0.0)
            spread.append(jnp.concatenate([one if g == kap // 4 else none for g in range(4)], axis=1))
        spread_ref[turn] = jnp.concatenate(spread, axis=0).astype(BF16)


def left_panel(l_ref, pick, mask, t_ref, a_ref):
    wide = []
    for u, (start, stop) in enumerate(SPANS):
        copies = jnp.dot(l_ref[:, start:stop], t_ref[AT[u] : AT[u + 1], :], preferred_element_type=F32)
        wide.append(copies.astype(BF16) * mask)
    for u in range(PAIRS):
        sums = jnp.dot(pick, wide[u], preferred_element_type=F32)
        hi = sums.astype(BF16)
        lo = (sums - hi.astype(F32)).astype(BF16)
        for h in range(2):
            i = 2 * u + h
            if i < BS:
                for g in range(KB // 4):
                    rows, lanes = slice(g * RB, (g + 1) * RB), slice(h * 128, (h + 1) * 128)
                    a_ref[i * RB : (i + 1) * RB, g * 128 : (g + 1) * 128] = hi[rows, lanes]
                    a_ref[i * RB : (i + 1) * RB, DEPTH + g * 128 : DEPTH + (g + 1) * 128] = lo[rows, lanes]


def right_panel(r_ref, spread_ref, w_ref, b_ref):
    w_ref[528:552, :] = jnp.zeros((24, 128), F32)
    w_ref[0:NB, :] = r_ref[...].astype(F32)
    pad = jnp.zeros((8, 128), F32)
    full = []
    for a in range(4):
        entries = []
        for q in range(QUADS):
            k = 4 * q + a
            if k < BS:
                entries += [w_ref[pl.ds(k, 24, stride=BS), :], pad]
            else:
                entries += [pad] * 4
        entries = jnp.concatenate(entries, axis=0).astype(BF16)
        full.append(jnp.dot(entries, spread_ref[a], preferred_element_type=F32))
    for q in range(QUADS):
        for g in range(4):
            v = [f[q * JP : q * JP + 24, g * 128 : (g + 1) * 128] for f in full]
            for a in range(4):
                z = jnp.concatenate([unrotate(v, a), pad], axis=0).astype(BF16)
                at = (4 * g + a) * JP
                b_ref[at : at + JP, q * 128 : (q + 1) * 128] = z


def product(panels, u):
    total = None
    for a, b in panels:
        for part in range(2):
            one = jnp.dot(a[:, part * DEPTH : (part + 1) * DEPTH], b[:, 256 * u : 256 * (u + 1)], preferred_element_type=F32)
            total = one if total is None else total + one
    return total


def put_rows(p_ref, add_ref, total, u):
    for i in range(BS):
        for h in range(2):
            part = total[i * RB : (i + 1) * RB, 128 * h : 128 * (h + 1)]
            at = (2 * u + h, pl.ds(i, RB, stride=24), slice(None))
            p_ref[at] = part if add_ref is None else part + add_ref[at]


def first_kernel(counts_hbm, rows_hbm, cols_hbm, kcols_hbm, l_hbm, r_hbm,
                 a_ref, b_ref, r_ref, t_ref, slots_ref, near_ref,
                 counts, rows, cols, kcols, l_ref, w_ref, spread_ref, sems):
    moves = [
        pltpu.make_async_copy(s, d, sems.at[n])
        for n, (s, d) in enumerate((
            (counts_hbm, counts), (rows_hbm, rows), (cols_hbm, cols), (kcols_hbm, kcols),
            (r_hbm, r_ref), (l_hbm, l_ref),
        ))
    ]
    for move in moves:
        move.start()
    spread_matrix(t_ref)
    for move in moves:
        move.wait()
    ncol, nrow = rows.shape[1], kcols.shape[0]
    for s in range(3):
        panel = lax.rem(lax.axis_index("col") + s, ncol)
        source = lax.rem(lax.axis_index("row") + s, nrow)
        panel_cols = cols[0, pl.ds(panel, 1), :]
        slots_ref[s : s + 1] = slot_code(rows[0, pl.ds(panel, 1), :], panel_cols, counts[0, panel])
        slots_ref[s + 3 : s + 4] = panel_cols
        near_ref[s] = kcols[source]
    column_spread(near_ref[0], spread_ref)
    right_panel(r_ref, spread_ref, w_ref, b_ref)
    left_panel(l_ref, slot_pick(slots_ref[0:1]), slot_mask(slots_ref[3:4]), t_ref, a_ref)


def relay_kernel(r0, r2, _, x_ref):
    odd = lax.rem(lax.axis_index("row"), 2)

    @pl.when(odd == 1)
    def _():
        x_ref[...] = r0[...]

    @pl.when(odd == 0)
    def _():
        x_ref[...] = r2[...]


def far_right_kernel(r, slots_ref, near_ref, a0, b0, _, b_ref, p_ref, pick_ref, mask_ref, near_spread_ref, w_ref, spread_ref):
    for s in (1, 2):
        pick_ref[s - 1] = slot_pick(slots_ref[s : s + 1])
        mask_ref[s - 1] = slot_mask(slots_ref[s + 3 : s + 4])
    column_spread(near_ref[1], near_spread_ref)
    column_spread(near_ref[2], spread_ref)
    right_panel(r, spread_ref, w_ref, b_ref)
    for u in range(3):
        put_rows(p_ref, None, product(((a0, b0),), u), u)


def last_kernel(l2, l1, r1, t_ref, pick_ref, mask_ref, spread_ref, b2, before_ref, out_hbm, a2, a1, b1, w_ref, p_ref, h_ref, o_ref, sems):
    left_panel(l2, pick_ref[1], mask_ref[1], t_ref, a2)
    left_panel(l1, pick_ref[0], mask_ref[0], t_ref, a1)
    right_panel(r1, spread_ref, w_ref, b1)
    out = out_hbm.reshape(NB * 4, 128)
    moves = []
    for u in range(3):
        put_rows(p_ref, before_ref, product(((a2, b2), (a1, b1)), u), u)
        for part in ((0, 1, 2),) if u < 2 else ((0,), (1,), (2,)):
            places = [(q, rq, ib) for ib in part for q in (2 * u, 2 * u + 1) for rq in range(RB // 4)]
            for q, rq, ib in places:
                at = [(4 * rq + a) * 24 + ib * 8 for a in range(4)]
                v = [p_ref[q, t : t + 8, :] for t in at]
                half = lanes_like(v[0]) < 64
                for a in (0, 1):
                    crossed = pltpu.roll(jnp.where(half, v[a + 2], v[a]), 64, 1)
                    h_ref[ib, q, rq, a] = jnp.where(half, v[a], crossed)
                    h_ref[ib, q, rq, a + 2] = jnp.where(half, crossed, v[a + 2])
            for q, rq, ib in places:
                n = 8 if ib < 2 else 7
                for a in (0, 2):
                    x, y = h_ref[ib, q, rq, a], h_ref[ib, q, rq, a + 1]
                    even = (lanes_like(x) & 32) == 0
                    z = (jnp.where(even, x, pltpu.roll(y, 32, 1)), jnp.where(even, pltpu.roll(x, 96, 1), y))
                    for b in range(2):
                        k = 4 * q + a + b
                        if k < BS:
                            o_ref[pl.ds((ib * 8 * BS + k) * 4 + rq, n, stride=4 * BS), :] = z[b][:n]
            if u == 2:
                rows = pl.ds(part[0] * 8 * BS * 4, (8 if part[0] < 2 else 7) * BS * 4)
                moves.append(pltpu.make_async_copy(o_ref.at[rows], out.at[rows], sems.at[part[0]]))
                moves[-1].start()
    for move in moves:
        move.wait()


VMEM = pl.BlockSpec(memory_space=pltpu.VMEM)
ANY = pl.BlockSpec(memory_space=pl.ANY)


def shape(*dims, dtype=F32):
    return jax.ShapeDtypeStruct(dims, dtype)


def call(kernel, flops, out_shape, in_specs, out_specs, scratch):
    return pl.pallas_call(
        kernel,
        out_shape=out_shape,
        in_specs=in_specs,
        out_specs=out_specs,
        scratch_shapes=scratch,
        compiler_params=pltpu.CompilerParams(vmem_limit_bytes=24 * 1024 * 1024),
        cost_estimate=pl.CostEstimate(flops=flops, bytes_accessed=1, transcendentals=0),
    )


def body(left_blocks, left_rows, left_cols, left_counts, right_blocks, right_cols):
    left = left_blocks[0, 0]
    right = jnp.swapaxes(right_blocks[0, 0], 0, 1)
    kcols = jnp.swapaxes(right_cols[:, 0], 1, 2)
    l2, l1 = from_behind(left, "col", -2), from_behind(left, "col", -1)
    r2 = from_behind(right, "row", -2)
    sums = shape(QUADS, RB * 24, 128)
    dense_left = shape(ROWS, 2 * DEPTH, dtype=BF16)
    dense_right = shape(DEPTH, WIDE, dtype=BF16)
    w_scratch = pltpu.VMEM((552, 128), F32)
    spread_scratch = pltpu.VMEM((4, KB * BPK, KB * CB), BF16)
    a0, b0, r0, spread_t, slots, near = call(
        first_kernel, 1,
        (
            dense_left, dense_right, shape(NB, 128, dtype=BF16), shape(AT[-1], 256, dtype=BF16),
            shape(8, SA, dtype=jnp.int32), shape(3, BPK, KB, dtype=jnp.int32),
        ),
        [ANY] * 6, (VMEM,) * 6,
        [
            pltpu.SMEM(left_counts.shape, jnp.int32),
            pltpu.VMEM(left_rows.shape, jnp.int32),
            pltpu.VMEM(left_cols.shape, jnp.int32),
            pltpu.VMEM(kcols.shape, jnp.int32),
            pltpu.VMEM((SA, NB), BF16),
            w_scratch, spread_scratch,
            pltpu.SemaphoreType.DMA((6,)),
        ],
    )(*(pltpu.with_memory_space_constraint(x, pltpu.HBM) for x in (left_counts, left_rows, left_cols, kcols, left, right)))
    relay = call(relay_kernel, 10**10, shape(NB, 128, dtype=BF16), [VMEM] * 2 + [ANY], VMEM, [])(r0, r2, a0)
    r1 = lax.ppermute(relay, "row", [(i, i ^ 1) for i in range(lax.axis_size("row"))])
    b2, before, pick, mask, near_spread = call(
        far_right_kernel, 10**10,
        (
            dense_right, sums, shape(2, 4 * RB, SA, dtype=BF16), shape(2, SA, 256, dtype=BF16),
            shape(*spread_scratch.shape, dtype=BF16),
        ),
        [VMEM] * 5 + [ANY], (VMEM,) * 5, [w_scratch, spread_scratch],
    )(r2, slots, near, a0, b0, relay)
    out = call(
        last_kernel, 10**10, shape(NB, 1, RB * CB), [VMEM] * 9, ANY,
        [
            pltpu.VMEM(dense_left.shape, BF16),
            pltpu.VMEM(dense_left.shape, BF16),
            pltpu.VMEM(dense_right.shape, BF16),
            w_scratch,
            pltpu.VMEM(sums.shape, F32),
            pltpu.VMEM((3, QUADS, 4, 4, 8, 128), F32),
            pltpu.VMEM((2120, 128), F32),
            pltpu.SemaphoreType.DMA((3,)),
        ],
    )(l2, l1, r1, spread_t, pick, mask, near_spread, b2, before)
    return jnp.transpose(out[None], (0, 2, 3, 1))


def solution(mesh):
    in_specs = (
        P("row", "col", None, None),
        P("row", None, None),
        P("row", None, None),
        P("row", None),
        P("row", "col", None, None),
        P(None, "col", None, None),
    )
    out_specs = P("row", "col", None, None)
    return jax.shard_map(body, mesh=mesh, in_specs=in_specs, out_specs=out_specs, check_vma=False)
```

```python
import jax
import jax.numpy as jnp
from jax import lax
from jax.experimental import pallas as pl
from jax.experimental.pallas import tpu as pltpu
from jax.sharding import PartitionSpec as P

BS = 23
RB = 16
CB = 32
KB = 16
BPK = 8
SA = 64
JP = 32
QUADS = 6
NB = BS * BS
ROWS = BS * RB
WIDE = QUADS * 128
DEPTH = KB * JP
PAIRS = 12
SPANS = tuple((46 * u // 128 * 128, min(-(-min(46 * u + 46, NB) // 128) * 128, NB)) for u in range(PAIRS))
SPANS = tuple((start, NB if stop > 512 else stop) for start, stop in SPANS)
AT = tuple(sum(stop - start for start, stop in SPANS[:u]) for u in range(PAIRS + 1))
F32 = jnp.float32
BF16 = jnp.bfloat16


def from_behind(value, axis, by):
    devices = lax.axis_size(axis)
    return lax.ppermute(value, axis, [(i, (i + by) % devices) for i in range(devices)])


def lanes_like(v):
    return lax.broadcasted_iota(jnp.int32, v.shape, 1)


def unrotate(v, shift):
    chunk = lanes_like(v[0]) >> 5
    z = v[(3 - shift) % 4]
    for p in range(3):
        z = jnp.where(chunk == p, v[(p - shift) % 4], z)
    return pltpu.roll(z, 128 - 32 * shift, 1) if shift else z


def spread_matrix(t_ref):
    for u, (start, stop) in enumerate(SPANS):
        lane = lax.broadcasted_iota(jnp.int32, (1, 256), 1)
        i, j = 2 * u + (lane >> 7), lane & 31
        source = jnp.where((j < BS) & (i < BS), i * BS + j, -1)
        entry = lax.broadcasted_iota(jnp.int32, (stop - start, 256), 0) + start
        t_ref[AT[u] : AT[u + 1], :] = jnp.where(entry == source, 1.0, 0.0).astype(BF16)


def slot_code(rows, cols, count):
    slot = lax.broadcasted_iota(jnp.int32, (1, SA), 1)
    return jnp.where(slot < count, (cols >> 2) * RB + rows, -1)


def slot_pick(code):
    place = lax.broadcasted_iota(jnp.int32, (4 * RB, SA), 0)
    return jnp.where(place == code, 1.0, 0.0).astype(BF16)


def slot_mask(cols):
    quarter = lax.broadcasted_iota(jnp.int32, (8, SA), 0)
    mine = jnp.where(quarter == (cols & 3), 1.0, 0.0)
    lane = lax.broadcasted_iota(jnp.int32, (8, 256), 1)
    quarter = lax.broadcasted_iota(jnp.int32, (8, 256), 0)
    chunk = jnp.where(quarter == ((lane >> 5) & 3), 1.0, 0.0)
    return lax.dot_general(mine, chunk, (((0,), (0,)), ((), ())), preferred_element_type=F32).astype(BF16)


def column_spread(cols, spread_ref):
    lane = lax.broadcasted_iota(jnp.int32, (BPK, 128), 1)
    none = jnp.zeros((BPK, 128), F32)
    hits = [(lane & 31) == cols[:, kap : kap + 1] for kap in range(KB)]
    for turn in range(4):
        spread = []
        for kap in range(KB):
            one = jnp.where(hits[kap] & ((lane >> 5) == (kap + turn) % 4), 1.0, 0.0)
            spread.append(jnp.concatenate([one if g == kap // 4 else none for g in range(4)], axis=1))
        spread_ref[turn] = jnp.concatenate(spread, axis=0).astype(BF16)


def left_panel(l_ref, pick, mask, t_ref, a_ref):
    wide = []
    for u, (start, stop) in enumerate(SPANS):
        copies = jnp.dot(l_ref[:, start:stop], t_ref[AT[u] : AT[u + 1], :], preferred_element_type=F32)
        wide.append(copies.astype(BF16) * mask)
    for u in range(PAIRS):
        sums = jnp.dot(pick, wide[u], preferred_element_type=F32)
        hi = sums.astype(BF16)
        lo = (sums - hi.astype(F32)).astype(BF16)
        for h in range(2):
            i = 2 * u + h
            if i < BS:
                for g in range(KB // 4):
                    rows, lanes = slice(g * RB, (g + 1) * RB), slice(h * 128, (h + 1) * 128)
                    a_ref[i * RB : (i + 1) * RB, g * 128 : (g + 1) * 128] = hi[rows, lanes]
                    a_ref[i * RB : (i + 1) * RB, DEPTH + g * 128 : DEPTH + (g + 1) * 128] = lo[rows, lanes]


def right_panel(r_ref, spread_ref, w_ref, b_ref):
    w_ref[528:552, :] = jnp.zeros((24, 128), F32)
    w_ref[0:NB, :] = r_ref[...].astype(F32)
    pad = jnp.zeros((8, 128), F32)
    full = []
    for a in range(4):
        entries = []
        for q in range(QUADS):
            k = 4 * q + a
            if k < BS:
                entries += [w_ref[pl.ds(k, 24, stride=BS), :], pad]
            else:
                entries += [pad] * 4
        entries = jnp.concatenate(entries, axis=0).astype(BF16)
        full.append(jnp.dot(entries, spread_ref[a], preferred_element_type=F32))
    for q in range(QUADS):
        for g in range(4):
            v = [f[q * JP : q * JP + 24, g * 128 : (g + 1) * 128] for f in full]
            for a in range(4):
                z = jnp.concatenate([unrotate(v, a), pad], axis=0).astype(BF16)
                at = (4 * g + a) * JP
                b_ref[at : at + JP, q * 128 : (q + 1) * 128] = z


def product(panels, u):
    total = None
    for a, b in panels:
        for part in range(2):
            one = jnp.dot(a[:, part * DEPTH : (part + 1) * DEPTH], b[:, 256 * u : 256 * (u + 1)], preferred_element_type=F32)
            total = one if total is None else total + one
    return total


def put_rows(p_ref, add_ref, total, u):
    for i in range(BS):
        for h in range(2):
            part = total[i * RB : (i + 1) * RB, 128 * h : 128 * (h + 1)]
            at = (2 * u + h, pl.ds(i, RB, stride=24), slice(None))
            p_ref[at] = part if add_ref is None else part + add_ref[at]


def first_kernel(counts_hbm, rows_hbm, cols_hbm, kcols_hbm, l_hbm, r_hbm,
                 a_ref, b_ref, r_ref, t_ref, slots_ref, near_ref,
                 counts, rows, cols, kcols, l_ref, w_ref, spread_ref, sems):
    moves = [
        pltpu.make_async_copy(s, d, sems.at[n])
        for n, (s, d) in enumerate((
            (counts_hbm, counts), (rows_hbm, rows), (cols_hbm, cols), (kcols_hbm, kcols),
            (r_hbm, r_ref), (l_hbm, l_ref),
        ))
    ]
    for move in moves:
        move.start()
    spread_matrix(t_ref)
    for move in moves:
        move.wait()
    ncol, nrow = rows.shape[1], kcols.shape[0]
    for s in range(3):
        panel = lax.rem(lax.axis_index("col") + s, ncol)
        source = lax.rem(lax.axis_index("row") + s, nrow)
        panel_cols = cols[0, pl.ds(panel, 1), :]
        slots_ref[s : s + 1] = slot_code(rows[0, pl.ds(panel, 1), :], panel_cols, counts[0, panel])
        slots_ref[s + 3 : s + 4] = panel_cols
        near_ref[s] = kcols[source]
    column_spread(near_ref[0], spread_ref)
    right_panel(r_ref, spread_ref, w_ref, b_ref)
    left_panel(l_ref, slot_pick(slots_ref[0:1]), slot_mask(slots_ref[3:4]), t_ref, a_ref)


def relay_kernel(r0, r2, _, x_ref):
    odd = lax.rem(lax.axis_index("row"), 2)

    @pl.when(odd == 1)
    def _():
        x_ref[...] = r0[...]

    @pl.when(odd == 0)
    def _():
        x_ref[...] = r2[...]


def far_right_kernel(r, slots_ref, near_ref, a0, b0, _, b_ref, p_ref, pick_ref, mask_ref, near_spread_ref, w_ref, spread_ref):
    column_spread(near_ref[2], spread_ref)
    right_panel(r, spread_ref, w_ref, b_ref)
    for u in range(3):
        put_rows(p_ref, None, product(((a0, b0),), u), u)
    for s in (1, 2):
        pick_ref[s - 1] = slot_pick(slots_ref[s : s + 1])
        mask_ref[s - 1] = slot_mask(slots_ref[s + 3 : s + 4])
    column_spread(near_ref[1], near_spread_ref)


def last_kernel(l2, l1, r1, t_ref, pick_ref, mask_ref, spread_ref, b2, before_ref, out_hbm, a2, a1, b1, w_ref, p_ref, h_ref, o_ref, sems):
    left_panel(l2, pick_ref[1], mask_ref[1], t_ref, a2)
    left_panel(l1, pick_ref[0], mask_ref[0], t_ref, a1)
    right_panel(r1, spread_ref, w_ref, b1)
    out = out_hbm.reshape(NB * 4, 128)
    moves = []
    for u in range(3):
        put_rows(p_ref, before_ref, product(((a2, b2), (a1, b1)), u), u)
        for part in ((0, 1, 2),) if u < 2 else ((0,), (1,), (2,)):
            places = [(q, rq, ib) for ib in part for q in (2 * u, 2 * u + 1) for rq in range(RB // 4)]
            for q, rq, ib in places:
                at = [(4 * rq + a) * 24 + ib * 8 for a in range(4)]
                v = [p_ref[q, t : t + 8, :] for t in at]
                half = lanes_like(v[0]) < 64
                for a in (0, 1):
                    crossed = pltpu.roll(jnp.where(half, v[a + 2], v[a]), 64, 1)
                    h_ref[ib, q, rq, a] = jnp.where(half, v[a], crossed)
                    h_ref[ib, q, rq, a + 2] = jnp.where(half, crossed, v[a + 2])
            for q, rq, ib in places:
                n = 8 if ib < 2 else 7
                for a in (0, 2):
                    x, y = h_ref[ib, q, rq, a], h_ref[ib, q, rq, a + 1]
                    even = (lanes_like(x) & 32) == 0
                    z = (jnp.where(even, x, pltpu.roll(y, 32, 1)), jnp.where(even, pltpu.roll(x, 96, 1), y))
                    for b in range(2):
                        k = 4 * q + a + b
                        if k < BS:
                            o_ref[pl.ds((ib * 8 * BS + k) * 4 + rq, n, stride=4 * BS), :] = z[b][:n]
            if u == 2:
                rows = pl.ds(part[0] * 8 * BS * 4, (8 if part[0] < 2 else 7) * BS * 4)
                moves.append(pltpu.make_async_copy(o_ref.at[rows], out.at[rows], sems.at[part[0]]))
                moves[-1].start()
    for move in moves:
        move.wait()


VMEM = pl.BlockSpec(memory_space=pltpu.VMEM)
ANY = pl.BlockSpec(memory_space=pl.ANY)


def shape(*dims, dtype=F32):
    return jax.ShapeDtypeStruct(dims, dtype)


def call(kernel, flops, out_shape, in_specs, out_specs, scratch):
    return pl.pallas_call(
        kernel,
        out_shape=out_shape,
        in_specs=in_specs,
        out_specs=out_specs,
        scratch_shapes=scratch,
        compiler_params=pltpu.CompilerParams(vmem_limit_bytes=24 * 1024 * 1024),
        cost_estimate=pl.CostEstimate(flops=flops, bytes_accessed=1, transcendentals=0),
    )


def body(left_blocks, left_rows, left_cols, left_counts, right_blocks, right_cols):
    left = left_blocks[0, 0]
    right = jnp.swapaxes(right_blocks[0, 0], 0, 1)
    kcols = jnp.swapaxes(right_cols[:, 0], 1, 2)
    l2, l1 = from_behind(left, "col", -2), from_behind(left, "col", -1)
    r2 = from_behind(right, "row", -2)
    sums = shape(QUADS, RB * 24, 128)
    dense_left = shape(ROWS, 2 * DEPTH, dtype=BF16)
    dense_right = shape(DEPTH, WIDE, dtype=BF16)
    w_scratch = pltpu.VMEM((552, 128), F32)
    spread_scratch = pltpu.VMEM((4, KB * BPK, KB * CB), BF16)
    a0, b0, r0, spread_t, slots, near = call(
        first_kernel, 1,
        (
            dense_left, dense_right, shape(NB, 128, dtype=BF16), shape(AT[-1], 256, dtype=BF16),
            shape(8, SA, dtype=jnp.int32), shape(3, BPK, KB, dtype=jnp.int32),
        ),
        [ANY] * 6, (VMEM,) * 6,
        [
            pltpu.SMEM(left_counts.shape, jnp.int32),
            pltpu.VMEM(left_rows.shape, jnp.int32),
            pltpu.VMEM(left_cols.shape, jnp.int32),
            pltpu.VMEM(kcols.shape, jnp.int32),
            pltpu.VMEM((SA, NB), BF16),
            w_scratch, spread_scratch,
            pltpu.SemaphoreType.DMA((6,)),
        ],
    )(*(pltpu.with_memory_space_constraint(x, pltpu.HBM) for x in (left_counts, left_rows, left_cols, kcols, left, right)))
    relay = call(relay_kernel, 10**10, shape(NB, 128, dtype=BF16), [VMEM] * 2 + [ANY], VMEM, [])(r0, r2, a0)
    r1 = lax.ppermute(relay, "row", [(i, i ^ 1) for i in range(lax.axis_size("row"))])
    b2, before, pick, mask, near_spread = call(
        far_right_kernel, 10**10,
        (
            dense_right, sums, shape(2, 4 * RB, SA, dtype=BF16), shape(2, SA, 256, dtype=BF16),
            shape(*spread_scratch.shape, dtype=BF16),
        ),
        [VMEM] * 5 + [ANY], (VMEM,) * 5, [w_scratch, spread_scratch],
    )(r2, slots, near, a0, b0, relay)
    out = call(
        last_kernel, 10**10, shape(NB, 1, RB * CB), [VMEM] * 9, ANY,
        [
            pltpu.VMEM(dense_left.shape, BF16),
            pltpu.VMEM(dense_left.shape, BF16),
            pltpu.VMEM(dense_right.shape, BF16),
            w_scratch,
            pltpu.VMEM(sums.shape, F32),
            pltpu.VMEM((3, QUADS, 4, 4, 8, 128), F32),
            pltpu.VMEM((2120, 128), F32),
            pltpu.SemaphoreType.DMA((3,)),
        ],
    )(l2, l1, r1, spread_t, pick, mask, near_spread, b2, before)
    return jnp.transpose(out[None], (0, 2, 3, 1))


def solution(mesh):
    in_specs = (
        P("row", "col", None, None),
        P("row", None, None),
        P("row", None, None),
        P("row", None),
        P("row", "col", None, None),
        P(None, "col", None, None),
    )
    out_specs = P("row", "col", None, None)
    return jax.shard_map(body, mesh=mesh, in_specs=in_specs, out_specs=out_specs, check_vma=False)
```

```python
import jax
import jax.numpy as jnp
from jax import lax
from jax.experimental import pallas as pl
from jax.experimental.pallas import tpu as pltpu
from jax.sharding import PartitionSpec as P

BS = 23
RB = 16
CB = 32
KB = 16
BPK = 8
SA = 64
JP = 32
QUADS = 6
NB = BS * BS
ROWS = BS * RB
WIDE = QUADS * 128
DEPTH = KB * JP
PAIRS = 12
SPANS = tuple((46 * u // 128 * 128, min(-(-min(46 * u + 46, NB) // 128) * 128, NB)) for u in range(PAIRS))
SPANS = tuple((start, NB if stop > 512 else stop) for start, stop in SPANS)
AT = tuple(sum(stop - start for start, stop in SPANS[:u]) for u in range(PAIRS + 1))
F32 = jnp.float32
BF16 = jnp.bfloat16


def from_behind(value, axis, by):
    devices = lax.axis_size(axis)
    return lax.ppermute(value, axis, [(i, (i + by) % devices) for i in range(devices)])


def lanes_like(v):
    return lax.broadcasted_iota(jnp.int32, v.shape, 1)


def unrotate(v, shift):
    chunk = lanes_like(v[0]) >> 5
    z = v[(3 - shift) % 4]
    for p in range(3):
        z = jnp.where(chunk == p, v[(p - shift) % 4], z)
    return pltpu.roll(z, 128 - 32 * shift, 1) if shift else z


def spread_matrix(t_ref):
    for u, (start, stop) in enumerate(SPANS):
        lane = lax.broadcasted_iota(jnp.int32, (1, 256), 1)
        i, j = 2 * u + (lane >> 7), lane & 31
        source = jnp.where((j < BS) & (i < BS), i * BS + j, -1)
        entry = lax.broadcasted_iota(jnp.int32, (stop - start, 256), 0) + start
        t_ref[AT[u] : AT[u + 1], :] = jnp.where(entry == source, 1.0, 0.0).astype(BF16)


def slot_code(rows, cols, count):
    slot = lax.broadcasted_iota(jnp.int32, (1, SA), 1)
    return jnp.where(slot < count, (cols >> 2) * RB + rows, -1)


def slot_pick(code):
    place = lax.broadcasted_iota(jnp.int32, (4 * RB, SA), 0)
    return jnp.where(place == code, 1.0, 0.0).astype(BF16)


def slot_mask(cols):
    quarter = lax.broadcasted_iota(jnp.int32, (8, SA), 0)
    mine = jnp.where(quarter == (cols & 3), 1.0, 0.0)
    lane = lax.broadcasted_iota(jnp.int32, (8, 256), 1)
    quarter = lax.broadcasted_iota(jnp.int32, (8, 256), 0)
    chunk = jnp.where(quarter == ((lane >> 5) & 3), 1.0, 0.0)
    return lax.dot_general(mine, chunk, (((0,), (0,)), ((), ())), preferred_element_type=F32).astype(BF16)


def column_spread(cols, spread_ref):
    lane = lax.broadcasted_iota(jnp.int32, (BPK, 128), 1)
    none = jnp.zeros((BPK, 128), F32)
    hits = [(lane & 31) == cols[:, kap : kap + 1] for kap in range(KB)]
    for turn in range(4):
        spread = []
        for kap in range(KB):
            one = jnp.where(hits[kap] & ((lane >> 5) == (kap + turn) % 4), 1.0, 0.0)
            spread.append(jnp.concatenate([one if g == kap // 4 else none for g in range(4)], axis=1))
        spread_ref[turn] = jnp.concatenate(spread, axis=0).astype(BF16)


def left_panel(l_ref, pick, mask, t_ref, a_ref):
    wide = []
    for u, (start, stop) in enumerate(SPANS):
        copies = jnp.dot(l_ref[:, start:stop], t_ref[AT[u] : AT[u + 1], :], preferred_element_type=F32)
        wide.append(copies.astype(BF16) * mask)
    for u in range(PAIRS):
        sums = jnp.dot(pick, wide[u], preferred_element_type=F32)
        hi = sums.astype(BF16)
        lo = (sums - hi.astype(F32)).astype(BF16)
        for h in range(2):
            i = 2 * u + h
            if i < BS:
                for g in range(KB // 4):
                    rows, lanes = slice(g * RB, (g + 1) * RB), slice(h * 128, (h + 1) * 128)
                    a_ref[i * RB : (i + 1) * RB, g * 128 : (g + 1) * 128] = hi[rows, lanes]
                    a_ref[i * RB : (i + 1) * RB, DEPTH + g * 128 : DEPTH + (g + 1) * 128] = lo[rows, lanes]


def right_panel(r_ref, spread_ref, w_ref, b_ref):
    w_ref[528:552, :] = jnp.zeros((24, 128), F32)
    w_ref[0:NB, :] = r_ref[...].astype(F32)
    pad = jnp.zeros((8, 128), F32)
    full = []
    for a in range(4):
        entries = []
        for q in range(QUADS):
            k = 4 * q + a
            if k < BS:
                entries += [w_ref[pl.ds(k, 24, stride=BS), :], pad]
            else:
                entries += [pad] * 4
        entries = jnp.concatenate(entries, axis=0).astype(BF16)
        full.append(jnp.dot(entries, spread_ref[a], preferred_element_type=F32))
    for q in range(QUADS):
        for g in range(4):
            v = [f[q * JP : q * JP + 24, g * 128 : (g + 1) * 128] for f in full]
            for a in range(4):
                z = jnp.concatenate([unrotate(v, a), pad], axis=0).astype(BF16)
                at = (4 * g + a) * JP
                b_ref[at : at + JP, q * 128 : (q + 1) * 128] = z


def product(panels, u):
    total = None
    for a, b in panels:
        for part in range(2):
            one = jnp.dot(a[:, part * DEPTH : (part + 1) * DEPTH], b[:, 256 * u : 256 * (u + 1)], preferred_element_type=F32)
            total = one if total is None else total + one
    return total


def put_rows(p_ref, add_ref, total, u):
    for i in range(BS):
        for h in range(2):
            part = total[i * RB : (i + 1) * RB, 128 * h : 128 * (h + 1)]
            at = (2 * u + h, pl.ds(i, RB, stride=24), slice(None))
            p_ref[at] = part if add_ref is None else part + add_ref[at]


def first_kernel(counts_hbm, rows_hbm, cols_hbm, kcols_hbm, l_hbm, r_hbm,
                 a_ref, b_ref, r_ref, t_ref, slots_ref, near_ref,
                 counts, rows, cols, kcols, l_ref, w_ref, spread_ref, sems):
    moves = [
        pltpu.make_async_copy(s, d, sems.at[n])
        for n, (s, d) in enumerate((
            (r_hbm, r_ref), (l_hbm, l_ref),
            (kcols_hbm, kcols), (cols_hbm, cols), (rows_hbm, rows), (counts_hbm, counts),
        ))
    ]
    for move in moves:
        move.start()
    spread_matrix(t_ref)
    for move in moves:
        move.wait()
    ncol, nrow = rows.shape[1], kcols.shape[0]
    for s in range(3):
        panel = lax.rem(lax.axis_index("col") + s, ncol)
        source = lax.rem(lax.axis_index("row") + s, nrow)
        panel_cols = cols[0, pl.ds(panel, 1), :]
        slots_ref[s : s + 1] = slot_code(rows[0, pl.ds(panel, 1), :], panel_cols, counts[0, panel])
        slots_ref[s + 3 : s + 4] = panel_cols
        near_ref[s] = kcols[source]
    column_spread(near_ref[0], spread_ref)
    right_panel(r_ref, spread_ref, w_ref, b_ref)
    left_panel(l_ref, slot_pick(slots_ref[0:1]), slot_mask(slots_ref[3:4]), t_ref, a_ref)


def relay_kernel(r0, r2, _, x_ref):
    odd = lax.rem(lax.axis_index("row"), 2)

    @pl.when(odd == 1)
    def _():
        x_ref[...] = r0[...]

    @pl.when(odd == 0)
    def _():
        x_ref[...] = r2[...]


def far_right_kernel(r, slots_ref, near_ref, a0, b0, _, b_ref, p_ref, pick_ref, mask_ref, near_spread_ref, w_ref, spread_ref):
    column_spread(near_ref[2], spread_ref)
    right_panel(r, spread_ref, w_ref, b_ref)
    for u in range(3):
        put_rows(p_ref, None, product(((a0, b0),), u), u)
    for s in (1, 2):
        pick_ref[s - 1] = slot_pick(slots_ref[s : s + 1])
        mask_ref[s - 1] = slot_mask(slots_ref[s + 3 : s + 4])
    column_spread(near_ref[1], near_spread_ref)


def last_kernel(l2, l1, r1, t_ref, pick_ref, mask_ref, spread_ref, b2, before_ref, out_hbm, a2, a1, b1, w_ref, p_ref, h_ref, o_ref, sems):
    left_panel(l2, pick_ref[1], mask_ref[1], t_ref, a2)
    left_panel(l1, pick_ref[0], mask_ref[0], t_ref, a1)
    right_panel(r1, spread_ref, w_ref, b1)
    out = out_hbm.reshape(NB * 4, 128)
    moves = []
    for u in range(3):
        put_rows(p_ref, before_ref, product(((a2, b2), (a1, b1)), u), u)
        for part in ((0, 1, 2),) if u < 2 else ((0,), (1,), (2,)):
            places = [(q, rq, ib) for ib in part for q in (2 * u, 2 * u + 1) for rq in range(RB // 4)]
            for q, rq, ib in places:
                at = [(4 * rq + a) * 24 + ib * 8 for a in range(4)]
                v = [p_ref[q, t : t + 8, :] for t in at]
                half = lanes_like(v[0]) < 64
                for a in (0, 1):
                    crossed = pltpu.roll(jnp.where(half, v[a + 2], v[a]), 64, 1)
                    h_ref[ib, q, rq, a] = jnp.where(half, v[a], crossed)
                    h_ref[ib, q, rq, a + 2] = jnp.where(half, crossed, v[a + 2])
            for q, rq, ib in places:
                n = 8 if ib < 2 else 7
                for a in (0, 2):
                    x, y = h_ref[ib, q, rq, a], h_ref[ib, q, rq, a + 1]
                    even = (lanes_like(x) & 32) == 0
                    z = (jnp.where(even, x, pltpu.roll(y, 32, 1)), jnp.where(even, pltpu.roll(x, 96, 1), y))
                    for b in range(2):
                        k = 4 * q + a + b
                        if k < BS:
                            o_ref[pl.ds((ib * 8 * BS + k) * 4 + rq, n, stride=4 * BS), :] = z[b][:n]
            if u == 2:
                rows = pl.ds(part[0] * 8 * BS * 4, (8 if part[0] < 2 else 7) * BS * 4)
                moves.append(pltpu.make_async_copy(o_ref.at[rows], out.at[rows], sems.at[part[0]]))
                moves[-1].start()
    for move in moves:
        move.wait()


VMEM = pl.BlockSpec(memory_space=pltpu.VMEM)
ANY = pl.BlockSpec(memory_space=pl.ANY)


def shape(*dims, dtype=F32):
    return jax.ShapeDtypeStruct(dims, dtype)


def call(kernel, flops, out_shape, in_specs, out_specs, scratch):
    return pl.pallas_call(
        kernel,
        out_shape=out_shape,
        in_specs=in_specs,
        out_specs=out_specs,
        scratch_shapes=scratch,
        compiler_params=pltpu.CompilerParams(vmem_limit_bytes=24 * 1024 * 1024),
        cost_estimate=pl.CostEstimate(flops=flops, bytes_accessed=1, transcendentals=0),
    )


def body(left_blocks, left_rows, left_cols, left_counts, right_blocks, right_cols):
    left = left_blocks[0, 0]
    right = jnp.swapaxes(right_blocks[0, 0], 0, 1)
    kcols = jnp.swapaxes(right_cols[:, 0], 1, 2)
    l2, l1 = from_behind(left, "col", -2), from_behind(left, "col", -1)
    r2 = from_behind(right, "row", -2)
    sums = shape(QUADS, RB * 24, 128)
    dense_left = shape(ROWS, 2 * DEPTH, dtype=BF16)
    dense_right = shape(DEPTH, WIDE, dtype=BF16)
    w_scratch = pltpu.VMEM((552, 128), F32)
    spread_scratch = pltpu.VMEM((4, KB * BPK, KB * CB), BF16)
    a0, b0, r0, spread_t, slots, near = call(
        first_kernel, 1,
        (
            dense_left, dense_right, shape(NB, 128, dtype=BF16), shape(AT[-1], 256, dtype=BF16),
            shape(8, SA, dtype=jnp.int32), shape(3, BPK, KB, dtype=jnp.int32),
        ),
        [ANY] * 6, (VMEM,) * 6,
        [
            pltpu.SMEM(left_counts.shape, jnp.int32),
            pltpu.VMEM(left_rows.shape, jnp.int32),
            pltpu.VMEM(left_cols.shape, jnp.int32),
            pltpu.VMEM(kcols.shape, jnp.int32),
            pltpu.VMEM((SA, NB), BF16),
            w_scratch, spread_scratch,
            pltpu.SemaphoreType.DMA((6,)),
        ],
    )(*(pltpu.with_memory_space_constraint(x, pltpu.HBM) for x in (left_counts, left_rows, left_cols, kcols, left, right)))
    relay = call(relay_kernel, 10**10, shape(NB, 128, dtype=BF16), [VMEM] * 2 + [ANY], VMEM, [])(r0, r2, a0)
    r1 = lax.ppermute(relay, "row", [(i, i ^ 1) for i in range(lax.axis_size("row"))])
    b2, before, pick, mask, near_spread = call(
        far_right_kernel, 10**10,
        (
            dense_right, sums, shape(2, 4 * RB, SA, dtype=BF16), shape(2, SA, 256, dtype=BF16),
            shape(*spread_scratch.shape, dtype=BF16),
        ),
        [VMEM] * 5 + [ANY], (VMEM,) * 5, [w_scratch, spread_scratch],
    )(r2, slots, near, a0, b0, relay)
    out = call(
        last_kernel, 10**10, shape(NB, 1, RB * CB), [VMEM] * 9, ANY,
        [
            pltpu.VMEM(dense_left.shape, BF16),
            pltpu.VMEM(dense_left.shape, BF16),
            pltpu.VMEM(dense_right.shape, BF16),
            w_scratch,
            pltpu.VMEM(sums.shape, F32),
            pltpu.VMEM((3, QUADS, 4, 4, 8, 128), F32),
            pltpu.VMEM((2120, 128), F32),
            pltpu.SemaphoreType.DMA((3,)),
        ],
    )(l2, l1, r1, spread_t, pick, mask, near_spread, b2, before)
    return jnp.transpose(out[None], (0, 2, 3, 1))


def solution(mesh):
    in_specs = (
        P("row", "col", None, None),
        P("row", None, None),
        P("row", None, None),
        P("row", None),
        P("row", "col", None, None),
        P(None, "col", None, None),
    )
    out_specs = P("row", "col", None, None)
    return jax.shard_map(body, mesh=mesh, in_specs=in_specs, out_specs=out_specs, check_vma=False)
```
